512 devices in a mesh: grp: 16 (over y_hi, x, core), dev: 32 (over z, y_lo).
Axes of the slice: x: 4, y: 8 (y_hi: 2, y_lo: 4; y = y_hi * 4 + y_lo), z: 8, core: 2. Of those that a mesh axis runs over, the one named last changes fastest.
Arguments:
- spectra: float32 [2048, 2, 2, 2048], P(('grp', 'dev')), may hold values from -120 to 120
- counts: int32 [2, 512], replicated, may hold values from 0 to 4
Outputs:
- correlations: bfloat16 [2, 2048, 128, 128], P(None, ('grp', 'dev'))
The draws below stay inside these ranges and needn't reach their ends.
Inputs may be any that keep to these rules, and one draw needn't show every extreme that they name: counts[s, b] live channels are the first ones of block b in segment s.
All inputs are finite; a program needn't handle non-finite values.
Results may differ from the reference program's by a relative error of at most 0.007.
Values may be sent and summed in bfloat16 or wider, within the bound.
A program may use at most 64 MiB of HBM per device.

```python
import math
import jax
import jax.numpy as jnp
from jax import lax

CH_DEV = 4
SEGS = 2
BINS = 2048
LAGS = 128
ROUNDS = 2
GROUP_CH = 128
CHANNELS = 2048
BLOCKS = 512
N_GRP = 16
N_DEV = 32


def draw_spectra(key, part):
    key = jax.random.fold_in(key, 11)
    subkeys = jax.random.split(key, 3)
    shape = (CHANNELS, SEGS, 2, BINS)
    basic_noise = jnp.clip(jax.random.normal(subkeys[0], shape, jnp.float32), -4.0, 4.0)
    channel_scale = jnp.exp(jax.random.uniform(subkeys[1], (CHANNELS, SEGS, 1, 1), jnp.float32, math.log(0.3), math.log(3.0)))
    bin_scale = jnp.exp(jax.random.uniform(subkeys[2], (1, 1, 1, BINS), jnp.float32, 0.0, math.log(10.0)))
    return (basic_noise * channel_scale * bin_scale).astype(jnp.float32)


def place_ends(values, rng, low, top_value):
    longest = values.shape.index(max(values.shape))
    spots = []
    for shift in (0, 1):
        where = [jax.random.randint(jax.random.fold_in(rng, axis), (), 0, length) for axis, length in enumerate(values.shape)]
        where[longest] = (where[longest] + shift) % values.shape[longest]
        spots.append(tuple(where))
    return values.at[spots[0]].set(low).at[spots[1]].set(top_value)


def setup_inputs(seed: int = 0) -> dict:
    streams_of = jax.random.split(jax.random.key(seed), 3)
    spectra = draw_spectra(jax.random.fold_in(streams_of[2], 71), 0)
    counts = place_ends(jax.random.randint(streams_of[1], (SEGS, BLOCKS), 0, CH_DEV + 1), jax.random.fold_in(streams_of[1], 1), 0, CH_DEV).astype(jnp.int32)
    return dict(spectra=spectra, counts=counts)


def valid_rows(counts, first_row, row_count, block_width):
    columns = lax.dynamic_slice_in_dim(counts, (first_row // block_width).astype(jnp.int32), row_count // block_width, 1)
    inside = jnp.arange(block_width, dtype=jnp.int32)
    is_live = inside[None, :, None] < jnp.transpose(columns)[:, None, :]
    return is_live.astype(jnp.float32).reshape(row_count, columns.shape[0])

def lag_table(bins_count, lags_count):
    frequency = jnp.arange(bins_count, dtype=jnp.int32)
    lag_index = jnp.arange(lags_count, dtype=jnp.int32) - lags_count // 2
    angles = jnp.mod(frequency[:, None] * lag_index[None, :], 2 * bins_count).astype(jnp.float32) * (math.pi / bins_count)
    table = jnp.concatenate([jnp.cos(angles), -jnp.sin(angles)], 0) / math.sqrt(bins_count)
    return table.astype(jnp.bfloat16)

def whiten(spectra, live):
    energy = lax.optimization_barrier(jnp.mean(spectra * spectra, axis=(2, 3)))
    return (spectra * (live / jnp.sqrt(energy + 1e-06))[:, :, None, None]).astype(jnp.bfloat16)

def pair_block(left_block, live_left, right_block, live_right, table):
    left_float = left_block.astype(jnp.float32)
    right_float = right_block.astype(jnp.float32)
    high = lax.Precision.HIGHEST
    real_part = jnp.einsum('isf,jsf->ijf', left_float[:, :, 0], right_float[:, :, 0], precision=high) + jnp.einsum('isf,jsf->ijf', left_float[:, :, 1], right_float[:, :, 1], precision=high)
    imag_part = jnp.einsum('isf,jsf->ijf', left_float[:, :, 1], right_float[:, :, 0], precision=high) - jnp.einsum('isf,jsf->ijf', left_float[:, :, 0], right_float[:, :, 1], precision=high)
    intersection = jnp.dot(live_left, jnp.transpose(live_right), precision=high)
    inverse = 1.0 / jnp.maximum(intersection, 1.0)
    stacked = (jnp.concatenate([real_part, imag_part], -1) * inverse[:, :, None]).astype(jnp.bfloat16)
    left_rows = left_block.shape[0]
    right_rows = right_block.shape[0]
    lagged = jnp.dot(stacked.reshape(left_rows * right_rows, -1), table, preferred_element_type=jnp.float32)
    return lagged.astype(jnp.bfloat16).reshape(left_rows, right_rows, -1)

def reference(spectra, counts):
    block_width = CH_DEV
    group_rows = GROUP_CH
    live = valid_rows(counts, jnp.int32(0), CHANNELS, block_width)
    whitened = whiten(spectra, live)
    table = lag_table(BINS, LAGS)
    stacked_rounds = []
    for offset in range(1, ROUNDS + 1):

        def single_block(block_index, offset=offset):
            group_index = block_index // N_DEV
            partner_group = jnp.mod(group_index - offset, N_GRP).astype(jnp.int32)
            left_block = lax.dynamic_slice_in_dim(whitened, (block_index * block_width).astype(jnp.int32), block_width, 0)
            live_left = lax.dynamic_slice_in_dim(live, (block_index * block_width).astype(jnp.int32), block_width, 0)
            right_block = lax.dynamic_slice_in_dim(whitened, (partner_group * group_rows).astype(jnp.int32), group_rows, 0)
            live_right = lax.dynamic_slice_in_dim(live, (partner_group * group_rows).astype(jnp.int32), group_rows, 0)
            return pair_block(left_block, live_left, right_block, live_right, table)
        lagged = lax.map(single_block, jnp.arange(BLOCKS, dtype=jnp.int32))
        stacked_rounds.append(lagged.reshape(CHANNELS, group_rows, LAGS))
    return jnp.stack(stacked_rounds, 0)
```

```python
import functools
import math

import jax
import jax.numpy as jnp
import ml_dtypes
import numpy as np
from jax import lax
from jax.experimental import pallas as pl
from jax.experimental.pallas import tpu as pltpu
from jax.sharding import PartitionSpec as P

LAGS = 128
ROUNDS = 2
NZ = 8
NY = 4
NG = 16
CH = 4
BINS = 2048
TILE = 128
MESH = pl.DeviceIdType.MESH


def lag_table():
    frequency = np.arange(BINS, dtype=np.int64)
    lag_index = np.arange(LAGS, dtype=np.int64) - LAGS // 2
    turns = np.mod(frequency[:, None] * lag_index[None, :], 2 * BINS)
    angles = turns * (math.pi / BINS)
    table = np.concatenate([np.cos(angles), -np.sin(angles)], 0) / math.sqrt(BINS)
    return table.astype(np.float32).astype(ml_dtypes.bfloat16)


def kernel(
    spectra_ref, counts_ref, table_ref, out_ref,
    raw, white, left, left_f32, right, partner, table, products, pieces,
    local_sem, left_send, left_recv, right_send, right_recv, pass_send, out_send, out_recv,
):
    g = lax.axis_index("grp")
    d = lax.axis_index("dev")
    z = d // NY
    y = d % NY
    core = g % 2

    load_raw = pltpu.make_async_copy(spectra_ref, raw, local_sem.at[0])
    load_raw.start()
    load_table = pltpu.make_async_copy(table_ref, table, local_sem.at[1])
    load_table.start()

    def ring(step):
        return (g, ((z + step + NZ) % NZ) * NY + y)

    def line(group_step, line_y):
        return ((g + group_step + NG) % NG, z * NY + line_y)

    barrier = pltpu.get_barrier_semaphore()

    def greet(device):
        pl.semaphore_signal(barrier, inc=1, device_id=device, device_id_type=MESH)

    for step in range(1, NZ):
        greet(ring(step))
    for other in range(NY):
        greet(line(-1, other))

    @pl.when(core == 0)
    def _():
        for other in range(NY):
            greet(line(-2, other))

    load_raw.wait()
    block = g * (NZ * NY) + d
    for ch in range(CH):
        for s in range(2):
            x = raw[ch, s]
            energy = jnp.sum(x * x) * (1.0 / (2 * BINS))
            live = jnp.where(counts_ref[s, block] > ch, 1.0, 0.0).astype(jnp.float32)
            scale = live / jnp.sqrt(jnp.full((1, BINS), energy + 1e-06, jnp.float32))
            left_f32[s * 8 + ch : s * 8 + ch + 1, :] = x[0:1] * scale
            left_f32[s * 8 + 4 + ch : s * 8 + 4 + ch + 1, :] = x[1:2] * scale
    white[...] = left_f32[...].astype(jnp.bfloat16)

    @pl.when(core == 0)
    def _():
        pl.semaphore_wait(barrier, NZ - 1 + 2 * NY)

    @pl.when(core == 1)
    def _():
        pl.semaphore_wait(barrier, NZ - 1 + NY)

    def left_copy(source, slot, step):
        return pltpu.make_async_remote_copy(
            src_ref=source, dst_ref=left.at[slot],
            send_sem=left_send.at[slot], recv_sem=left_recv.at[slot],
            device_id=ring(step), device_id_type=MESH,
        )

    def half_copy(source_slot, half, step):
        columns = pl.ds(half * (BINS // 2), BINS // 2)
        return pltpu.make_async_remote_copy(
            src_ref=left.at[source_slot, :, columns], dst_ref=left.at[NZ - 1, :, columns],
            send_sem=left_send.at[NZ - 1 + half], recv_sem=left_recv.at[NZ - 1 + half],
            device_id=ring(step), device_id_type=MESH,
        )

    def right_copy(k, other):
        return pltpu.make_async_remote_copy(
            src_ref=white, dst_ref=right.at[k, y],
            send_sem=right_send.at[k, other], recv_sem=right_recv.at[k, y],
            device_id=line(k + 1, other), device_id_type=MESH,
        )

    def right_arrival(k, other):
        return pltpu.make_async_remote_copy(
            src_ref=white, dst_ref=right.at[k, other],
            send_sem=right_send.at[k, other], recv_sem=right_recv.at[k, other],
            device_id=line(k + 1, other), device_id_type=MESH,
        )

    def pass_copy(other):
        return pltpu.make_async_remote_copy(
            src_ref=right.at[0, other], dst_ref=right.at[1, other],
            send_sem=pass_send.at[other], recv_sem=right_recv.at[1, other],
            device_id=line(1, y), device_id_type=MESH,
        )

    left_copy(white, 1, 1).start()
    left_copy(white, 2, -1).start()
    for other in range(NY):
        right_copy(0, other).start()

    @pl.when(core == 0)
    def _():
        for other in range(NY):
            right_copy(1, other).start()

    for n in range(1, NZ // 2):
        for slot, step in ((2 * n - 1, 1), (2 * n, -1)):
            left_copy(white, slot, step).wait_recv()
            if n < NZ // 2 - 1:
                left_copy(left.at[slot], slot + 2, step).start()
            else:
                half_copy(slot, (1 - step) // 2, step).start()
    for other in range(NY):
        right_arrival(0, other).wait_recv()

        @pl.when(core == 0)
        def _():
            pass_copy(other).start()

    def gather(k):
        def body(t, carry):
            columns = pl.ds(pl.multiple_of(t * TILE, TILE), TILE)
            parts = [right[k, other, :, columns].astype(jnp.float32) for other in range(NY)]
            for sc in range(4):
                rows = jnp.concatenate([p[4 * sc : 4 * sc + 4] for p in parts], axis=0)
                partner[k, sc, :, columns] = rows.astype(jnp.bfloat16)
            return carry

        lax.fori_loop(0, BINS // TILE, body, 0)

    gather(0)
    for other in range(NY):
        right_arrival(1, other).wait_recv()
    gather(1)
    load_table.wait()

    row = lax.broadcasted_iota(jnp.int32, (NY * CH, LAGS), 0)
    both = []
    for k in range(ROUNDS):
        partner_first = ((g - 1 - k + NG) % NG) * (NZ * NY) + z * NY
        limit = jnp.zeros((NY * CH, LAGS), jnp.int32)
        for other in range(NY):
            least = jnp.minimum(
                counts_ref[0, partner_first + other], counts_ref[1, partner_first + other]
            )
            limit = jnp.where(row // CH == other, least, limit)
        both.append(jnp.where(row % CH < limit, 0.5, 0.0).astype(jnp.float32))

    def out_copy(slot, other_slot, owner_z, land_z):
        return pltpu.make_async_remote_copy(
            src_ref=pieces.at[slot],
            dst_ref=out_ref.at[:, :, pl.ds(pl.multiple_of(land_z * 16, 16), 16), :],
            send_sem=out_send.at[slot], recv_sem=out_recv.at[other_slot],
            device_id=(g, owner_z * NY + y), device_id_type=MESH,
        )

    def mate(slot):
        return jnp.where(slot == NZ - 1, slot, jnp.where(slot % 2 == 1, slot + 1, slot - 1))

    def source_z(slot):
        step = jnp.where(slot % 2 == 1, NZ - (slot + 1) // 2, slot // 2)
        return (z + step) % NZ

    def one_block(slot, carry):
        @pl.when(slot == NZ - 1)
        def _():
            half_copy(1, 0, 1).wait_recv()
            half_copy(2, 1, -1).wait_recv()

        @pl.when(slot == 0)
        def _():
            left_f32[...] = white[...].astype(jnp.float32)

        @pl.when(slot > 0)
        def _():
            left_f32[...] = left[slot].astype(jnp.float32)

        def tile(t, inner):
            at = pl.multiple_of(t * TILE, TILE)
            columns = pl.ds(at, TILE)
            imag_columns = pl.ds(pl.multiple_of(BINS + at, TILE), TILE)
            theirs = [[partner[k, sc, :, columns] for sc in range(4)] for k in range(ROUNDS)]
            for ch in range(CH):
                mine = [
                    jnp.broadcast_to(
                        left_f32[4 * sc + ch : 4 * sc + ch + 1, columns], (16, TILE)
                    ).astype(jnp.bfloat16)
                    for sc in range(4)
                ]
                for k in range(ROUNDS):
                    a0, b0, a1, b1 = theirs[k]
                    ma0, mb0, ma1, mb1 = mine
                    real = (ma0 * a0 + mb0 * b0) + (ma1 * a1 + mb1 * b1)
                    imag = (mb0 * a0 - ma0 * b0) + (mb1 * a1 - ma1 * b1)
                    at_row = (k * CH + ch) * 16
                    products[at_row : at_row + 16, columns] = real
                    products[at_row : at_row + 16, imag_columns] = imag
            return inner

        lax.fori_loop(0, BINS // TILE, tile, 0)
        lagged = jnp.dot(products[...], table[...], preferred_element_type=jnp.float32)
        owner = source_z(slot)
        mine_block = g * (NZ * NY) + owner * NY + y
        least = jnp.minimum(counts_ref[0, mine_block], counts_ref[1, mine_block])
        for ch in range(CH):
            factor = jnp.where(least > ch, 1.0, 0.0).astype(jnp.float32)
            for k in range(ROUNDS):
                at_row = (k * CH + ch) * 16
                scale = 1.0 - both[k] * factor
                pieces[slot, k, ch] = (lagged[at_row : at_row + 16] * scale).astype(jnp.bfloat16)

        @pl.when(slot == 0)
        def _():
            pltpu.make_async_copy(
                pieces.at[0],
                out_ref.at[:, :, pl.ds(pl.multiple_of(z * 16, 16), 16), :],
                local_sem.at[2],
            ).start()

        @pl.when(slot > 0)
        def _():
            out_copy(slot, mate(slot), owner, z).start()

        return carry

    lax.fori_loop(0, NZ, one_block, 0)

    def finish(slot, carry):
        out_copy(slot, slot, source_z(slot), source_z(slot)).wait_recv()
        out_copy(slot, slot, source_z(slot), source_z(slot)).wait_send()
        return carry

    lax.fori_loop(1, NZ, finish, 0)
    pltpu.make_async_copy(
        pieces.at[0],
        out_ref.at[:, :, pl.ds(pl.multiple_of(z * 16, 16), 16), :],
        local_sem.at[2],
    ).wait()
    for slot in range(1, NZ - 1):
        left_copy(white, slot, 1).wait_send()
    half_copy(1, 0, 1).wait_send()
    half_copy(2, 1, -1).wait_send()
    for other in range(NY):
        right_copy(0, other).wait_send()

    @pl.when(core == 0)
    def _():
        for other in range(NY):
            right_copy(1, other).wait_send()
            pass_copy(other).wait_send()


def local(spectra, counts, table):
    bf16 = jnp.bfloat16
    dma = pltpu.SemaphoreType.DMA
    return pl.pallas_call(
        kernel,
        out_shape=jax.ShapeDtypeStruct((ROUNDS, CH, NZ * NY * CH, LAGS), bf16),
        in_specs=[
            pl.BlockSpec(memory_space=pl.ANY),
            pl.BlockSpec(memory_space=pltpu.SMEM),
            pl.BlockSpec(memory_space=pl.ANY),
        ],
        out_specs=pl.BlockSpec(memory_space=pl.ANY),
        scratch_shapes=[
            pltpu.VMEM((CH, 2, 2, BINS), jnp.float32),
            pltpu.VMEM((16, BINS), bf16),
            pltpu.VMEM((NZ, 16, BINS), bf16),
            pltpu.VMEM((16, BINS), jnp.float32),
            pltpu.VMEM((ROUNDS, NY, 16, BINS), bf16),
            pltpu.VMEM((ROUNDS, 4, 16, BINS), bf16),
            pltpu.VMEM((2 * BINS, LAGS), bf16),
            pltpu.VMEM((ROUNDS * CH * 16, 2 * BINS), bf16),
            pltpu.VMEM((NZ, ROUNDS, CH, 16, LAGS), bf16),
            dma((3,)),
            dma((NZ + 1,)),
            dma((NZ + 1,)),
            dma((ROUNDS, NY)),
            dma((ROUNDS, NY)),
            dma((NY,)),
            dma((NZ,)),
            dma((NZ,)),
        ],
        compiler_params=pltpu.CompilerParams(
            collective_id=0, has_side_effects=True, vmem_limit_bytes=32 * 1024 * 1024
        ),
        cost_estimate=pl.CostEstimate(
            flops=1100000000, bytes_accessed=1600000, transcendentals=0
        ),
    )(spectra, counts, table)


def solution(mesh):
    table = lag_table()

    def whole(spectra, counts):
        return jax.shard_map(
            local,
            mesh=mesh,
            in_specs=(P(("grp", "dev"), None, None, None), P(), P()),
            out_specs=P(None, ("grp", "dev"), None, None),
            check_vma=False,
        )(spectra, counts, jnp.asarray(table))

    return whole
```

```python
import math

import jax
import jax.numpy as jnp
import ml_dtypes
import numpy as np
from jax import lax
from jax.experimental import pallas as pl
from jax.experimental.pallas import tpu as pltpu
from jax.sharding import PartitionSpec as P

LAGS = 128
ROUNDS = 2
NZ = 8
NY = 4
NG = 16
NX = 4
CH = 4
BINS = 2048
TILE = 128
TILES = BINS // TILE
PEERS = 2 * NY
MESH = pl.DeviceIdType.MESH


def lag_table():
    frequency = np.arange(BINS, dtype=np.int64)
    lag_index = np.arange(LAGS, dtype=np.int64) - LAGS // 2
    turns = np.mod(frequency[:, None] * lag_index[None, :], 2 * BINS)
    angles = turns * (math.pi / BINS)
    table = np.stack([np.cos(angles), -np.sin(angles)], 0) / math.sqrt(BINS)
    table = table.reshape(2, TILES, TILE, LAGS).transpose(1, 0, 2, 3).reshape(2 * BINS, LAGS)
    return table.astype(np.float32).astype(ml_dtypes.bfloat16)


def kernel(
    spectra_ref, counts_hbm, table_ref, out_ref,
    raw, counts, white, wide_f32, left, left_wide, right, partner, table, pieces, landed, result,
    local_sem, late_sem, left_send, left_recv, right_recv, import_send, along_send, mate_send,
    out_send, out_recv,
):
    g = lax.axis_index("grp")
    d = lax.axis_index("dev")
    z = d // NY
    y = d % NY
    core = g % 2
    x = (g // 2) % NX
    parity = z % 2
    q = z // 2
    late = q >= 2
    me = parity * NY + y
    mate_g = g + 1 - 2 * core

    load_raw = pltpu.make_async_copy(spectra_ref, raw, local_sem.at[0])
    load_raw.start()
    load_counts = pltpu.make_async_copy(counts_hbm, counts, local_sem.at[1])
    load_counts.start()
    load_table = pltpu.make_async_copy(table_ref, table, local_sem.at[2])
    load_table.start()

    def peer(slot):
        return (g, (2 * q + slot // NY) * NY + slot % NY)

    def row(other_q, group):
        return (group, (parity + 2 * other_q) * NY + y)

    beside = q + 1 - 2 * (q % 2)
    far = [(q + 2) % 4, (beside + 2) % 4]
    mate = (mate_g, d)
    mirrored = z * NY + (NY - 1 - y)
    import_to = ((g + 2) % NG, jnp.where(x == NX - 1, mirrored, d))
    import_from = ((g - 2 + NG) % NG, jnp.where(x == 0, mirrored, d))

    barrier = pltpu.get_barrier_semaphore()

    def greet(device, semaphore=barrier):
        pl.semaphore_signal(semaphore, inc=1, device_id=device, device_id_type=MESH)

    @pl.when(jnp.logical_not(late))
    def _():
        for other in far:
            greet(row(other, g))
            greet(row(other, mate_g))

    greet(import_from)
    for step in range(1, PEERS):
        greet(peer((me + step) % PEERS))
    greet(mate)
    greet(row(beside, g))
    greet(row(beside, mate_g))

    near = 1 + (PEERS - 1) + 1 + 2

    load_counts.wait()
    load_raw.wait()
    block = g * (NZ * NY) + d
    for ch in range(CH):
        for s in range(2):
            values = raw[ch, s]
            energy = jnp.sum(values * values) * (1.0 / (2 * BINS))
            live = jnp.where(counts[s, block] > ch, 1.0, 0.0).astype(jnp.float32)
            scale = live / jnp.sqrt(jnp.full((1, BINS), energy + 1e-06, jnp.float32))
            wide_f32[s * 8 + ch : s * 8 + ch + 1, :] = values[0:1] * scale
            wide_f32[s * 8 + 4 + ch : s * 8 + 4 + ch + 1, :] = values[1:2] * scale
    white[...] = wide_f32[...].astype(jnp.bfloat16)

    @pl.when(jnp.logical_not(late))
    def _():
        pl.semaphore_wait(barrier, near)

    @pl.when(late)
    def _():
        pl.semaphore_wait(barrier, near + 4)
        for other in far:
            greet(row(other, g), late_sem)
            greet(row(other, mate_g), late_sem)

    def import_copy():
        return pltpu.make_async_remote_copy(
            src_ref=white, dst_ref=right.at[1, q],
            send_sem=import_send, recv_sem=right_recv.at[1, q],
            device_id=import_to, device_id_type=MESH,
        )

    def along_copy(n, other):
        return pltpu.make_async_remote_copy(
            src_ref=right.at[1, q], dst_ref=right.at[1, q],
            send_sem=along_send.at[n], recv_sem=right_recv.at[1, q],
            device_id=row(other, g), device_id_type=MESH,
        )

    def own_copy(n, other):
        return pltpu.make_async_remote_copy(
            src_ref=white, dst_ref=right.at[0, q],
            send_sem=mate_send.at[n], recv_sem=right_recv.at[0, q],
            device_id=row(other, mate_g), device_id_type=MESH,
        )

    def mate_copy(n, other):
        return pltpu.make_async_remote_copy(
            src_ref=right.at[1, other], dst_ref=right.at[0, other],
            send_sem=mate_send.at[n], recv_sem=right_recv.at[0, other],
            device_id=mate, device_id_type=MESH,
        )

    def arrival(k, other):
        return pltpu.make_async_remote_copy(
            src_ref=white, dst_ref=right.at[k, other],
            send_sem=import_send, recv_sem=right_recv.at[k, other],
            device_id=mate, device_id_type=MESH,
        )

    def left_copy(n, slot):
        return pltpu.make_async_remote_copy(
            src_ref=white, dst_ref=left.at[me],
            send_sem=left_send.at[n], recv_sem=left_recv.at[me],
            device_id=peer(slot), device_id_type=MESH,
        )

    def left_arrival(slot):
        return pltpu.make_async_remote_copy(
            src_ref=white, dst_ref=left.at[slot],
            send_sem=left_send.at[0], recv_sem=left_recv.at[slot],
            device_id=peer(slot), device_id_type=MESH,
        )

    import_copy().start()

    @pl.when(jnp.logical_and(core == 0, late))
    def _():
        own_copy(2, far[0]).start()
        own_copy(3, far[1]).start()

    @pl.when(core == 0)
    def _():
        own_copy(0, q).start()
        own_copy(1, beside).start()

    for n in range(PEERS - 1):
        left_copy(n, (me + 1 + n) % PEERS).start()

    arrival(1, q).wait_recv()

    @pl.when(late)
    def _():
        along_copy(1, far[0]).start()
        along_copy(2, far[1]).start()

    along_copy(0, beside).start()

    @pl.when(core == 1)
    def _():
        mate_copy(0, q).start()

    @pl.when(jnp.logical_not(late))
    def _():
        pl.semaphore_wait(late_sem, 4)

        @pl.when(core == 0)
        def _():
            own_copy(2, far[0]).start()
            own_copy(3, far[1]).start()

        along_copy(1, far[0]).start()
        along_copy(2, far[1]).start()

    def widen(n, carry):
        slot = (me + n) % PEERS

        @pl.when(n > 0)
        def _():
            left_arrival(slot).wait_recv()
            wide_f32[...] = left[slot].astype(jnp.float32)

        def tile(t, inner):
            columns = pl.ds(pl.multiple_of(t * TILE, TILE), TILE)
            for r in range(16):
                left_wide[slot * 16 + r, :, columns] = jnp.broadcast_to(
                    wide_f32[r : r + 1, columns], (16, TILE)
                ).astype(jnp.bfloat16)
            return inner

        lax.fori_loop(0, TILES, tile, 0)
        return carry

    lax.fori_loop(0, PEERS, widen, 0)
    load_table.wait()

    mirror = x == 0
    flip = [jnp.logical_and(mirror, core == 0), mirror]
    row_id = lax.broadcasted_iota(jnp.int32, (16, LAGS), 0)

    def out_copy(e, n, slot):
        return pltpu.make_async_remote_copy(
            src_ref=pieces.at[e, slot], dst_ref=landed.at[e, me],
            send_sem=out_send.at[e, n], recv_sem=out_recv.at[e, me],
            device_id=peer(slot), device_id_type=MESH,
        )

    def out_arrival(e, slot):
        return pltpu.make_async_remote_copy(
            src_ref=pieces.at[e, slot], dst_ref=landed.at[e, slot],
            send_sem=out_send.at[e, 0], recv_sem=out_recv.at[e, slot],
            device_id=peer(slot), device_id_type=MESH,
        )

    def half(e, carry):
        for zz in range(2):
            other = 2 * e + zz

            @pl.when(other != q)
            def _():
                arrival(1, other).wait_recv()

                @pl.when(core == 1)
                def _():
                    mate_copy((other - q + 4) % 4, other).start()

        for zz in range(2):
            arrival(0, 2 * e + zz).wait_recv()

        def gather(t, inner):
            columns = pl.ds(pl.multiple_of(t * TILE, TILE), TILE)
            parts = [
                right[k, 2 * e + zz, :, columns].astype(jnp.float32)
                for k in range(ROUNDS)
                for zz in range(2)
            ]
            for sc in range(4):
                rows = jnp.concatenate([p[4 * sc : 4 * sc + 4] for p in parts], axis=0)
                partner[sc, :, columns] = rows.astype(jnp.bfloat16)
            return inner

        lax.fori_loop(0, TILES, gather, 0)

        limit = jnp.zeros((16, LAGS), jnp.int32)
        for k in range(ROUNDS):
            column = jnp.where(flip[k], NY - 1 - y, y)
            for zz in range(2):
                group = (g - 1 - k + NG) % NG
                at = group * (NZ * NY) + (parity + 2 * (2 * e + zz)) * NY + column
                least = jnp.minimum(counts[0, at], counts[1, at])
                limit = jnp.where(row_id // 4 == k * 2 + zz, least, limit)
        both = jnp.where(row_id % 4 < limit, 0.5, 0.0).astype(jnp.float32)

        def owners(n, inner):
            slots = [(me + 1 + 2 * n + i) % PEERS for i in range(2)]

            def tile(t, acc):
                columns = pl.ds(pl.multiple_of(t * TILE, TILE), TILE)
                a0, b0, a1, b1 = [partner[sc, :, columns] for sc in range(4)]
                products = []
                for slot in slots:
                    for ch in range(CH):
                        ma0, mb0, ma1, mb1 = [
                            left_wide[slot * 16 + 4 * sc + ch, :, columns] for sc in range(4)
                        ]
                        real = (ma0 * a0 + mb0 * b0) + (ma1 * a1 + mb1 * b1)
                        imag = (mb0 * a0 - ma0 * b0) + (mb1 * a1 - ma1 * b1)
                        products.append(jnp.concatenate([real, imag], axis=1))
                rows = pl.ds(pl.multiple_of(t * 2 * TILE, 2 * TILE), 2 * TILE)
                return acc + jnp.dot(
                    jnp.concatenate(products, axis=0),
                    table[rows, :],
                    preferred_element_type=jnp.float32,
                )

            lagged = lax.fori_loop(
                0, TILES, tile, jnp.zeros((2 * CH * 16, LAGS), jnp.float32), unroll=2
            )
            for i, slot in enumerate(slots):
                at = g * (NZ * NY) + (2 * q + slot // NY) * NY + slot % NY
                least = jnp.minimum(counts[0, at], counts[1, at])
                for ch in range(CH):
                    factor = jnp.where(least > ch, 1.0, 0.0).astype(jnp.float32)
                    first = (i * CH + ch) * 16
                    pieces[e, slot, ch] = (
                        lagged[first : first + 16] * (1.0 - both * factor)
                    ).astype(jnp.bfloat16)
            out_copy(e, 2 * n, slots[0]).start()

            @pl.when(n < PEERS // 2 - 1)
            def _():
                out_copy(e, 2 * n + 1, slots[1]).start()

            return inner

        lax.fori_loop(0, PEERS // 2, owners, 0)
        return carry

    lax.fori_loop(0, 2, half, 0)

    def store(e):
        return pltpu.make_async_copy(
            result.at[:, :, pl.ds(e * 64, 64), :],
            out_ref.at[:, :, pl.ds(e * 64, 64), :],
            local_sem.at[3 + e],
        )

    for e in range(2):
        for n in range(PEERS - 1):
            out_arrival(e, (me + 1 + n) % PEERS).wait_recv()
        landed[e, me] = pieces[e, me]

        def assemble(n, carry, e=e):
            side = n // CH
            ch = n % CH
            for k in range(ROUNDS):
                parts = []
                for column in range(NY):
                    source = jnp.where(flip[k], NY - 1 - column, column)
                    tile = landed[e, side * NY + source, ch].astype(jnp.float32)
                    parts.append(tile[8 * k : 8 * k + 8])
                for zz in range(2):
                    rows = jnp.concatenate([p[4 * zz : 4 * zz + 4] for p in parts], axis=0)
                    at = pl.multiple_of((side + 4 * e + 2 * zz) * 16, 16)
                    result[k, ch, pl.ds(at, 16), :] = rows.astype(jnp.bfloat16)
            return carry

        lax.fori_loop(0, 2 * CH, assemble, 0)
        store(e).start()

    import_copy().wait_send()
    for n in range(PEERS - 1):
        left_copy(n, (me + 1 + n) % PEERS).wait_send()
        for e in range(2):
            out_copy(e, n, (me + 1 + n) % PEERS).wait_send()
    along_copy(0, beside).wait_send()
    along_copy(1, far[0]).wait_send()
    along_copy(2, far[1]).wait_send()

    @pl.when(core == 0)
    def _():
        own_copy(0, q).wait_send()
        own_copy(1, beside).wait_send()
        own_copy(2, far[0]).wait_send()
        own_copy(3, far[1]).wait_send()

    @pl.when(core == 1)
    def _():
        for n in range(4):
            mate_copy(n, (q + n) % 4).wait_send()

    store(0).wait()
    store(1).wait()


def local(spectra, counts, table):
    bf16 = jnp.bfloat16
    dma = pltpu.SemaphoreType.DMA
    return pl.pallas_call(
        kernel,
        out_shape=jax.ShapeDtypeStruct((ROUNDS, CH, NZ * NY * CH, LAGS), bf16),
        in_specs=[pl.BlockSpec(memory_space=pl.ANY)] * 3,
        out_specs=pl.BlockSpec(memory_space=pl.ANY),
        scratch_shapes=[
            pltpu.VMEM((CH, 2, 2, BINS), jnp.float32),
            pltpu.SMEM(counts.shape, jnp.int32),
            pltpu.VMEM((16, BINS), bf16),
            pltpu.VMEM((16, BINS), jnp.float32),
            pltpu.VMEM((PEERS, 16, BINS), bf16),
            pltpu.VMEM((PEERS * 16, 16, BINS), bf16),
            pltpu.VMEM((ROUNDS, 4, 16, BINS), bf16),
            pltpu.VMEM((4, 16, BINS), bf16),
            pltpu.VMEM((2 * BINS, LAGS), bf16),
            pltpu.VMEM((2, PEERS, CH, 16, LAGS), bf16),
            pltpu.VMEM((2, PEERS, CH, 16, LAGS), bf16),
            pltpu.VMEM((ROUNDS, CH, NZ * NY * CH, LAGS), bf16),
            dma((5,)),
            pltpu.SemaphoreType.REGULAR,
            dma((PEERS - 1,)),
            dma((PEERS,)),
            dma((ROUNDS, 4)),
            dma,
            dma((3,)),
            dma((4,)),
            dma((2, PEERS - 1)),
            dma((2, PEERS)),
        ],
        compiler_params=pltpu.CompilerParams(
            collective_id=0, has_side_effects=True, vmem_limit_bytes=60 * 1024 * 1024
        ),
        cost_estimate=pl.CostEstimate(
            flops=1100000000, bytes_accessed=1600000, transcendentals=0
        ),
    )(spectra, counts, table)


def solution(mesh):
    table = lag_table()

    def whole(spectra, counts):
        return jax.shard_map(
            local,
            mesh=mesh,
            in_specs=(P(("grp", "dev"), None, None, None), P(), P()),
            out_specs=P(None, ("grp", "dev"), None, None),
            check_vma=False,
        )(spectra, counts, jnp.asarray(table))

    return whole
```

```python
import math

import jax
import jax.numpy as jnp
import ml_dtypes
import numpy as np
from jax import lax
from jax.experimental import pallas as pl
from jax.experimental.pallas import tpu as pltpu
from jax.sharding import PartitionSpec as P

LAGS = 128
ROUNDS = 2
NZ = 8
NY = 4
NG = 16
NX = 4
CH = 4
BINS = 2048
TILE = 256
TILES = BINS // TILE
PEERS = 2 * NY
OWNERS = 4
MESH = pl.DeviceIdType.MESH


def lag_table():
    frequency = np.arange(BINS, dtype=np.int64)
    lag_index = np.arange(LAGS, dtype=np.int64) - LAGS // 2
    turns = np.mod(frequency[:, None] * lag_index[None, :], 2 * BINS)
    angles = turns * (math.pi / BINS)
    table = np.stack([np.cos(angles), -np.sin(angles)], 0) / math.sqrt(BINS)
    table = table.reshape(2, TILES, TILE, LAGS).transpose(1, 0, 2, 3).reshape(2 * BINS, LAGS)
    return table.astype(np.float32).astype(ml_dtypes.bfloat16)


def kernel(
    spectra_ref, counts_hbm, table_ref, out_ref,
    raw, counts, white, wide_f32, left, left_wide, right, partner, table, pieces, landed, result,
    local_sem, reply_sem, left_send, left_recv, right_recv, ahead_send, mate_send,
    out_send, out_recv,
):
    g = lax.axis_index("grp")
    d = lax.axis_index("dev")
    z = d // NY
    y = d % NY
    core = g % 2
    x = (g // 2) % NX
    parity = z % 2
    q = z // 2
    me = parity * NY + y
    mate_g = g + 1 - 2 * core

    load_raw = pltpu.make_async_copy(spectra_ref, raw, local_sem.at[0])
    load_raw.start()
    load_counts = pltpu.make_async_copy(counts_hbm, counts, local_sem.at[1])
    load_counts.start()
    load_table = pltpu.make_async_copy(table_ref, table, local_sem.at[2])
    load_table.start()

    def peer(slot):
        return (g, (2 * q + slot // NY) * NY + slot % NY)

    def row(other_q, group):
        return (group, (parity + 2 * other_q) * NY + y)

    mate = (mate_g, d)
    column_to = jnp.where(x == NX - 1, NY - 1 - y, y)
    column_from = jnp.where(x == 0, NY - 1 - y, y)

    def ahead(other_q):
        return ((g + 2) % NG, (parity + 2 * other_q) * NY + column_to)

    def behind(other_q):
        return ((g - 2 + NG) % NG, (parity + 2 * other_q) * NY + column_from)

    barrier = pltpu.get_barrier_semaphore()

    def greet(device, semaphore=barrier):
        pl.semaphore_signal(semaphore, inc=1, device_id=device, device_id_type=MESH)

    for other in range(1, 4):

        @pl.when(other > q)
        def _():
            greet(behind(other))
            greet(ahead(other))
            greet(row(other, mate_g))

    greet(behind(q))
    greet(mate)
    for step in range(1, PEERS):
        greet(peer((me + step) % PEERS))

    load_counts.wait()
    load_raw.wait()
    block = g * (NZ * NY) + d
    for ch in range(CH):
        for s in range(2):
            values = raw[ch, s]
            square = values * values
            lanes = square[:, 0:128]
            for t in range(1, BINS // 128):
                lanes = lanes + square[:, t * 128 : (t + 1) * 128]
            total = jnp.sum(jnp.sum(lanes, axis=0, keepdims=True), axis=1, keepdims=True)
            live = jnp.where(counts[s, block] > ch, 1.0, 0.0).astype(jnp.float32)
            scale = live / jnp.sqrt(total * (1.0 / (2 * BINS)) + 1e-06)
            wide_f32[s * 8 + ch : s * 8 + ch + 1, :] = values[0:1] * scale
            wide_f32[s * 8 + 4 + ch : s * 8 + 4 + ch + 1, :] = values[1:2] * scale
    white[...] = wide_f32[...].astype(jnp.bfloat16)

    pl.semaphore_wait(barrier, PEERS + 1 + 3 * q)
    for other in range(3):

        @pl.when(other < q)
        def _():
            greet(behind(other), reply_sem.at[q])
            greet(row(other, mate_g), reply_sem.at[q])

    def ahead_copy(n, other):
        return pltpu.make_async_remote_copy(
            src_ref=white, dst_ref=right.at[1, q],
            send_sem=ahead_send.at[n], recv_sem=right_recv.at[1, q],
            device_id=ahead(other), device_id_type=MESH,
        )

    def own_copy(n, other):
        return pltpu.make_async_remote_copy(
            src_ref=white, dst_ref=right.at[0, q],
            send_sem=mate_send.at[n], recv_sem=right_recv.at[0, q],
            device_id=row(other, mate_g), device_id_type=MESH,
        )

    def mate_copy(n, other):
        return pltpu.make_async_remote_copy(
            src_ref=right.at[1, other], dst_ref=right.at[0, other],
            send_sem=mate_send.at[n], recv_sem=right_recv.at[0, other],
            device_id=mate, device_id_type=MESH,
        )

    def arrival(k, other):
        return pltpu.make_async_remote_copy(
            src_ref=white, dst_ref=right.at[k, other],
            send_sem=ahead_send.at[0], recv_sem=right_recv.at[k, other],
            device_id=mate, device_id_type=MESH,
        )

    facing = (PEERS // 2 + me) % PEERS

    def left_copy(source, slot, target, n):
        return pltpu.make_async_remote_copy(
            src_ref=source, dst_ref=left.at[slot],
            send_sem=left_send.at[n], recv_sem=left_recv.at[slot],
            device_id=peer(target), device_id_type=MESH,
        )

    def in_row(n):
        return parity * NY + (y + n) % NY

    def send_row(other):
        ahead_copy(other, other).start()

        @pl.when(core == 0)
        def _():
            own_copy(other, other).start()

    for other in range(3):

        @pl.when(other < q)
        def _():
            send_row(other)

    for n in range(1, NY):
        left_copy(white, me, in_row(n), n).start()
    left_copy(white, me, facing, 0).start()
    send_row(q)

    def left_arrival(slot):
        left_copy(white, slot, facing, 0).wait_recv()

    for n in range(1, NY):
        left_arrival(in_row(n))
        left_copy(left.at[in_row(n)], in_row(n), facing, NY - 1 + n).start()

    for other in range(1, 4):

        @pl.when(other > q)
        def _():
            pl.semaphore_wait(reply_sem.at[other], 2)
            send_row(other)

    def widen(n, carry):
        row_first = jnp.where(n < NY, parity, 1 - parity) * NY
        slot = row_first + (y + n) % NY

        @pl.when(n >= NY)
        def _():
            left_arrival(slot)

        @pl.when(n > 0)
        def _():
            wide_f32[...] = left[slot].astype(jnp.float32)

        def tile(t, inner):
            columns = pl.ds(pl.multiple_of(t * TILE, TILE), TILE)
            for r in range(16):
                left_wide[slot * 16 + r, :, columns] = jnp.broadcast_to(
                    wide_f32[r : r + 1, columns], (16, TILE)
                ).astype(jnp.bfloat16)
            return inner

        lax.fori_loop(0, TILES, tile, 0)
        return carry

    lax.fori_loop(0, PEERS, widen, 0)
    load_table.wait()

    mirror = x == 0
    flip = [jnp.logical_and(mirror, core == 0), mirror]
    row_id = lax.broadcasted_iota(jnp.int32, (16, LAGS), 0)

    def out_copy(e, n, slot):
        return pltpu.make_async_remote_copy(
            src_ref=pieces.at[e, slot], dst_ref=landed.at[e, me],
            send_sem=out_send.at[e, n], recv_sem=out_recv.at[e, me],
            device_id=peer(slot), device_id_type=MESH,
        )

    def out_arrival(e, slot):
        return pltpu.make_async_remote_copy(
            src_ref=pieces.at[e, slot], dst_ref=landed.at[e, slot],
            send_sem=out_send.at[e, 0], recv_sem=out_recv.at[e, slot],
            device_id=peer(slot), device_id_type=MESH,
        )

    def half(turn, carry):
        e = (q // 2 + turn) % 2
        for zz in range(2):
            other = 2 * e + zz

            arrival(1, other).wait_recv()

            @pl.when(core == 1)
            def _():
                mate_copy(other, other).start()

        for zz in range(2):
            arrival(0, 2 * e + zz).wait_recv()

        def gather(t, inner):
            columns = pl.ds(pl.multiple_of(t * TILE, TILE), TILE)
            parts = [
                right[k, 2 * e + zz, :, columns].astype(jnp.float32)
                for k in range(ROUNDS)
                for zz in range(2)
            ]
            for sc in range(4):
                rows = jnp.concatenate([p[4 * sc : 4 * sc + 4] for p in parts], axis=0)
                partner[sc, :, columns] = rows.astype(jnp.bfloat16)
            return inner

        lax.fori_loop(0, TILES, gather, 0)

        limit = jnp.zeros((16, LAGS), jnp.int32)
        for k in range(ROUNDS):
            column = jnp.where(flip[k], NY - 1 - y, y)
            for zz in range(2):
                group = (g - 1 - k + NG) % NG
                at = group * (NZ * NY) + (parity + 2 * (2 * e + zz)) * NY + column
                least = jnp.minimum(counts[0, at], counts[1, at])
                limit = jnp.where(row_id // 4 == k * 2 + zz, least, limit)
        both = jnp.where(row_id % 4 < limit, 0.5, 0.0).astype(jnp.float32)

        def owners(n, inner):
            pair = (y // 2 + 1 + n) % 2
            slots = [(i // 2) * NY + pair * 2 + i % 2 for i in range(OWNERS)]

            def tile(t, acc):
                columns = pl.ds(pl.multiple_of(t * TILE, TILE), TILE)
                a0, b0, a1, b1 = [partner[sc, :, columns] for sc in range(4)]
                products = []
                for slot in slots:
                    for ch in range(CH):
                        ma0, mb0, ma1, mb1 = [
                            left_wide[slot * 16 + 4 * sc + ch, :, columns] for sc in range(4)
                        ]
                        real = (ma0 * a0 + mb0 * b0) + (ma1 * a1 + mb1 * b1)
                        imag = (mb0 * a0 - ma0 * b0) + (mb1 * a1 - ma1 * b1)
                        products.append(jnp.concatenate([real, imag], axis=1))
                rows = pl.ds(pl.multiple_of(t * 2 * TILE, 2 * TILE), 2 * TILE)
                return acc + jnp.dot(
                    jnp.concatenate(products, axis=0),
                    table[rows, :],
                    preferred_element_type=jnp.float32,
                )

            lagged = lax.fori_loop(
                0, TILES, tile, jnp.zeros((OWNERS * CH * 16, LAGS), jnp.float32), unroll=TILES
            )
            for i, slot in enumerate(slots):
                at = g * (NZ * NY) + (2 * q + slot // NY) * NY + slot % NY
                least = jnp.minimum(counts[0, at], counts[1, at])
                for ch in range(CH):
                    factor = jnp.where(least > ch, 1.0, 0.0).astype(jnp.float32)
                    first = (i * CH + ch) * 16
                    pieces[e, slot, ch] = (
                        lagged[first : first + 16] * (1.0 - both * factor)
                    ).astype(jnp.bfloat16)
            for i, slot in enumerate(slots):

                @pl.when(slot != me)
                def _():
                    out_copy(e, slot, slot).start()

            return inner

        lax.fori_loop(0, PEERS // OWNERS, owners, 0)
        return carry

    lax.fori_loop(0, 2, half, 0)

    def store(e):
        return pltpu.make_async_copy(
            result.at[:, :, pl.ds(pl.multiple_of(e * 64, 64), 64), :],
            out_ref.at[:, :, pl.ds(pl.multiple_of(e * 64, 64), 64), :],
            local_sem.at[3 + e],
        )

    for turn in range(2):
        e = (q // 2 + turn) % 2
        for n in range(PEERS - 1):
            out_arrival(e, (me + 1 + n) % PEERS).wait_recv()
        landed[e, me] = pieces[e, me]

        def assemble(n, carry, e=e):
            side = n // CH
            ch = n % CH
            for k in range(ROUNDS):
                parts = []
                for column in range(NY):
                    source = jnp.where(flip[k], NY - 1 - column, column)
                    tile = landed[e, side * NY + source, ch].astype(jnp.float32)
                    parts.append(tile[8 * k : 8 * k + 8])
                for zz in range(2):
                    rows = jnp.concatenate([p[4 * zz : 4 * zz + 4] for p in parts], axis=0)
                    at = pl.multiple_of((side + 4 * e + 2 * zz) * 16, 16)
                    result[k, ch, pl.ds(at, 16), :] = rows.astype(jnp.bfloat16)
            return carry

        lax.fori_loop(0, 2 * CH, assemble, 0)
        store(e).start()

    for n in range(PEERS - 1):
        left_copy(white, me, facing, n).wait_send()
        for e in range(2):
            out_copy(e, (me + 1 + n) % PEERS, facing).wait_send()
    for other in range(4):
        ahead_copy(other, other).wait_send()

        @pl.when(core == 0)
        def _():
            own_copy(other, other).wait_send()

        @pl.when(core == 1)
        def _():
            mate_copy(other, other).wait_send()

    store(0).wait()
    store(1).wait()


def local(spectra, counts, table):
    bf16 = jnp.bfloat16
    dma = pltpu.SemaphoreType.DMA
    return pl.pallas_call(
        kernel,
        out_shape=jax.ShapeDtypeStruct((ROUNDS, CH, NZ * NY * CH, LAGS), bf16),
        in_specs=[pl.BlockSpec(memory_space=pl.ANY)] * 3,
        out_specs=pl.BlockSpec(memory_space=pl.ANY),
        scratch_shapes=[
            pltpu.VMEM((CH, 2, 2, BINS), jnp.float32),
            pltpu.SMEM(counts.shape, jnp.int32),
            pltpu.VMEM((16, BINS), bf16),
            pltpu.VMEM((16, BINS), jnp.float32),
            pltpu.VMEM((PEERS, 16, BINS), bf16),
            pltpu.VMEM((PEERS * 16, 16, BINS), bf16),
            pltpu.VMEM((ROUNDS, 4, 16, BINS), bf16),
            pltpu.VMEM((4, 16, BINS), bf16),
            pltpu.VMEM((2 * BINS, LAGS), bf16),
            pltpu.VMEM((2, PEERS, CH, 16, LAGS), bf16),
            pltpu.VMEM((2, PEERS, CH, 16, LAGS), bf16),
            pltpu.VMEM((ROUNDS, CH, NZ * NY * CH, LAGS), bf16),
            dma((5,)),
            pltpu.SemaphoreType.REGULAR((4,)),
            dma((PEERS - 1,)),
            dma((PEERS,)),
            dma((ROUNDS, 4)),
            dma((4,)),
            dma((4,)),
            dma((2, PEERS)),
            dma((2, PEERS)),
        ],
        compiler_params=pltpu.CompilerParams(
            collective_id=0, has_side_effects=True, vmem_limit_bytes=60 * 1024 * 1024
        ),
        cost_estimate=pl.CostEstimate(
            flops=1100000000, bytes_accessed=1600000, transcendentals=0
        ),
    )(spectra, counts, table)


def solution(mesh):
    table = lag_table()

    def whole(spectra, counts):
        return jax.shard_map(
            local,
            mesh=mesh,
            in_specs=(P(("grp", "dev"), None, None, None), P(), P()),
            out_specs=P(None, ("grp", "dev"), None, None),
            check_vma=False,
        )(spectra, counts, jnp.asarray(table))

    return whole
```

```python
import math

import jax
import jax.numpy as jnp
import ml_dtypes
import numpy as np
from jax import lax
from jax.experimental import pallas as pl
from jax.experimental.pallas import tpu as pltpu
from jax.sharding import PartitionSpec as P

LAGS = 128
ROUNDS = 2
NZ = 8
NY = 4
NG = 16
NX = 4
CH = 4
BINS = 2048
TILE = 512
TILES = BINS // TILE
PEERS = 2 * NY
OWNERS = 4
MESH = pl.DeviceIdType.MESH


def lag_table():
    frequency = np.arange(BINS, dtype=np.int64)
    lag_index = np.arange(LAGS, dtype=np.int64) - LAGS // 2
    turns = np.mod(frequency[:, None] * lag_index[None, :], 2 * BINS)
    angles = turns * (math.pi / BINS)
    table = np.stack([np.cos(angles), -np.sin(angles)], 0) / math.sqrt(BINS)
    table = table.reshape(2, TILES, TILE, LAGS).transpose(1, 0, 2, 3).reshape(2 * BINS, LAGS)
    return table.astype(np.float32).astype(ml_dtypes.bfloat16)


def kernel(
    spectra_ref, counts_hbm, table_ref, out_ref,
    raw, counts, white, fed, wide_f32, left, left_wide, right, partner, table, pieces, landed, result,
    local_sem, reply_sem, left_send, left_recv, right_recv, ahead_send, feed_sem, spread_send, mate_send,
    out_send, out_recv,
):
    g = lax.axis_index("grp")
    d = lax.axis_index("dev")
    z = d // NY
    y = d % NY
    core = g % 2
    x = (g // 2) % NX
    parity = z % 2
    q = z // 2
    me = parity * NY + y
    mate_g = g + 1 - 2 * core

    load_raw = pltpu.make_async_copy(spectra_ref, raw, local_sem.at[0])
    load_raw.start()
    load_counts = pltpu.make_async_copy(counts_hbm, counts, local_sem.at[1])
    load_counts.start()
    load_table = pltpu.make_async_copy(table_ref, table, local_sem.at[2])
    load_table.start()

    def peer(slot):
        return (g, (2 * q + slot // NY) * NY + slot % NY)

    def row(other_q, group):
        return (group, (parity + 2 * other_q) * NY + y)

    late = q >= 2
    beside = q + 1 - 2 * (q % 2)
    mate = (mate_g, d)
    column_to = jnp.where(x == NX - 1, NY - 1 - y, y)
    column_from = jnp.where(x == 0, NY - 1 - y, y)

    def ahead(other_q):
        return ((g + 2) % NG, (parity + 2 * other_q) * NY + column_to)

    feeds = jnp.logical_and(x == NX - 1, core == 0)
    spreads = jnp.logical_and(x == 0, core == 0)
    fed_by = ((g + 6) % NG, d)
    feed_to = ((g + 10) % NG, d)

    def behind(other_q):
        group = jnp.where(spreads, g + 8, g - 2 + NG) % NG
        return (group, (parity + 2 * other_q) * NY + column_from)

    barrier = pltpu.get_barrier_semaphore()

    def greet(device, semaphore=barrier):
        pl.semaphore_signal(semaphore, inc=1, device_id=device, device_id_type=MESH)

    @pl.when(jnp.logical_not(late))
    def _():
        for other in (2, 3):
            greet(behind(other))
            greet(row(other, mate_g))

        @pl.when(jnp.logical_not(feeds))
        def _():
            for other in (2, 3):
                greet(ahead(other))

    @pl.when(spreads)
    def _():
        greet(fed_by)

    greet(behind(q))
    greet(behind(beside))
    greet(mate)
    greet(row(beside, mate_g))
    for step in range(1, PEERS):
        greet(peer((me + step) % PEERS))
    near = 4 + PEERS - 1 + jnp.where(spreads, 2, 0) - jnp.where(feeds, 1, 0)

    load_counts.wait()
    load_raw.wait()
    block = g * (NZ * NY) + d
    for ch in range(CH):
        for s in range(2):
            values = raw[ch, s]
            square = values * values
            lanes = square[:, 0:128]
            for t in range(1, BINS // 128):
                lanes = lanes + square[:, t * 128 : (t + 1) * 128]
            total = jnp.sum(jnp.sum(lanes, axis=0, keepdims=True), axis=1, keepdims=True)
            live = jnp.where(counts[s, block] > ch, 1.0, 0.0).astype(jnp.float32)
            scale = live / jnp.sqrt(total * (1.0 / (2 * BINS)) + 1e-06)
            wide_f32[s * 8 + ch : s * 8 + ch + 1, :] = values[0:1] * scale
            wide_f32[s * 8 + 4 + ch : s * 8 + 4 + ch + 1, :] = values[1:2] * scale
    white[...] = wide_f32[...].astype(jnp.bfloat16)

    @pl.when(jnp.logical_not(late))
    def _():
        pl.semaphore_wait(barrier, near)

    @pl.when(late)
    def _():
        pl.semaphore_wait(barrier, near + 6 - jnp.where(feeds, 2, 0))
        for other in (0, 1):
            greet(behind(other), reply_sem.at[q])
            greet(row(other, mate_g), reply_sem.at[q])

    def ahead_copy(n, other):
        return pltpu.make_async_remote_copy(
            src_ref=white, dst_ref=right.at[1, q],
            send_sem=ahead_send.at[n], recv_sem=right_recv.at[1, q],
            device_id=ahead(other), device_id_type=MESH,
        )

    def own_copy(n, other):
        return pltpu.make_async_remote_copy(
            src_ref=white, dst_ref=right.at[0, q],
            send_sem=mate_send.at[n], recv_sem=right_recv.at[0, q],
            device_id=row(other, mate_g), device_id_type=MESH,
        )

    def mate_copy(n, other):
        return pltpu.make_async_remote_copy(
            src_ref=right.at[1, other], dst_ref=right.at[0, other],
            send_sem=mate_send.at[n], recv_sem=right_recv.at[0, other],
            device_id=mate, device_id_type=MESH,
        )

    def arrival(k, other):
        return pltpu.make_async_remote_copy(
            src_ref=white, dst_ref=right.at[k, other],
            send_sem=ahead_send.at[0], recv_sem=right_recv.at[k, other],
            device_id=mate, device_id_type=MESH,
        )

    facing = (PEERS // 2 + me) % PEERS

    def left_copy(source, slot, target, n):
        return pltpu.make_async_remote_copy(
            src_ref=source, dst_ref=left.at[slot],
            send_sem=left_send.at[n], recv_sem=left_recv.at[slot],
            device_id=peer(target), device_id_type=MESH,
        )

    def in_row(n):
        flipped = y + 1 - 2 * (y % 2)
        return parity * NY + (flipped if n == 1 else (y + 2) % NY if n == 2 else (flipped + 2) % NY)

    def feed_copy():
        return pltpu.make_async_remote_copy(
            src_ref=white, dst_ref=fed, send_sem=feed_sem.at[0], recv_sem=feed_sem.at[1],
            device_id=feed_to, device_id_type=MESH,
        )

    def spread_copy(other):
        return pltpu.make_async_remote_copy(
            src_ref=fed, dst_ref=right.at[1, q],
            send_sem=spread_send.at[other], recv_sem=right_recv.at[1, q],
            device_id=behind(other), device_id_type=MESH,
        )

    def send_row(other):
        @pl.when(jnp.logical_not(feeds))
        def _():
            ahead_copy(other, other).start()

        @pl.when(core == 0)
        def _():
            own_copy(other, other).start()

    @pl.when(feeds)
    def _():
        feed_copy().start()

    @pl.when(late)
    def _():
        for other in (0, 1):
            send_row(other)

    send_row(q)
    send_row(beside)
    for n in range(1, NY):
        left_copy(white, me, in_row(n), n).start()
    left_copy(white, me, facing, 0).start()

    def left_arrival(slot):
        left_copy(white, slot, facing, 0).wait_recv()

    @pl.when(spreads)
    def _():
        feed_copy().wait_recv()

        @pl.when(late)
        def _():
            spread_copy(0).start()
            spread_copy(1).start()

        spread_copy(q).start()
        spread_copy(beside).start()

    for n in range(1, NY):
        left_arrival(in_row(n))
        left_copy(left.at[in_row(n)], in_row(n), facing, NY - 1 + n).start()

    for other in (q, beside):
        arrival(1, other).wait_recv()

        @pl.when(core == 1)
        def _():
            mate_copy(other, other).start()

    @pl.when(jnp.logical_not(late))
    def _():
        for other in (2, 3):
            pl.semaphore_wait(
                reply_sem.at[other], 2 + jnp.where(spreads, 1, 0) - jnp.where(feeds, 1, 0)
            )
            send_row(other)

            @pl.when(spreads)
            def _():
                spread_copy(other).start()

    def widen(n, carry):
        row_first = jnp.where(n < NY, parity, 1 - parity) * NY
        slot = row_first + (y + n) % NY

        @pl.when(n >= NY)
        def _():
            left_arrival(slot)

        @pl.when(n > 0)
        def _():
            wide_f32[...] = left[slot].astype(jnp.float32)

        def tile(t, inner):
            columns = pl.ds(pl.multiple_of(t * TILE, TILE), TILE)
            for r in range(16):
                left_wide[slot * 16 + r, :, columns] = jnp.broadcast_to(
                    wide_f32[r : r + 1, columns], (16, TILE)
                ).astype(jnp.bfloat16)
            return inner

        lax.fori_loop(0, TILES, tile, 0)
        return carry

    lax.fori_loop(0, PEERS, widen, 0)
    load_table.wait()

    mirror = x == 0
    flip = [jnp.logical_and(mirror, core == 0), mirror]
    row_id = lax.broadcasted_iota(jnp.int32, (16, LAGS), 0)

    def out_copy(e, n, slot):
        return pltpu.make_async_remote_copy(
            src_ref=pieces.at[e, slot], dst_ref=landed.at[e, me],
            send_sem=out_send.at[e, n], recv_sem=out_recv.at[e, me],
            device_id=peer(slot), device_id_type=MESH,
        )

    def out_arrival(e, slot):
        return pltpu.make_async_remote_copy(
            src_ref=pieces.at[e, slot], dst_ref=landed.at[e, slot],
            send_sem=out_send.at[e, 0], recv_sem=out_recv.at[e, slot],
            device_id=peer(slot), device_id_type=MESH,
        )

    def half(turn, carry):
        e = (q // 2 + turn) % 2
        @pl.when(turn == 1)
        def _():
            for zz in range(2):
                arrival(1, 2 * e + zz).wait_recv()

                @pl.when(core == 1)
                def _():
                    mate_copy(2 * e + zz, 2 * e + zz).start()

        for zz in range(2):
            arrival(0, 2 * e + zz).wait_recv()

        def gather(t, inner):
            columns = pl.ds(pl.multiple_of(t * TILE, TILE), TILE)
            parts = [
                right[k, 2 * e + zz, :, columns].astype(jnp.float32)
                for k in range(ROUNDS)
                for zz in range(2)
            ]
            for sc in range(4):
                rows = jnp.concatenate([p[4 * sc : 4 * sc + 4] for p in parts], axis=0)
                partner[sc, :, columns] = rows.astype(jnp.bfloat16)
            return inner

        lax.fori_loop(0, TILES, gather, 0)

        limit = jnp.zeros((16, LAGS), jnp.int32)
        for k in range(ROUNDS):
            column = jnp.where(flip[k], NY - 1 - y, y)
            for zz in range(2):
                group = (g - 1 - k + NG) % NG
                at = group * (NZ * NY) + (parity + 2 * (2 * e + zz)) * NY + column
                least = jnp.minimum(counts[0, at], counts[1, at])
                limit = jnp.where(row_id // 4 == k * 2 + zz, least, limit)
        both = jnp.where(row_id % 4 < limit, 0.5, 0.0).astype(jnp.float32)

        def owners(n, inner):
            pair = (y // 2 + 1 + n) % 2
            slots = [(i // 2) * NY + pair * 2 + i % 2 for i in range(OWNERS)]

            def tile(t, acc):
                columns = pl.ds(pl.multiple_of(t * TILE, TILE), TILE)
                a0, b0, a1, b1 = [partner[sc, :, columns] for sc in range(4)]
                products = []
                for slot in slots:
                    for ch in range(CH):
                        ma0, mb0, ma1, mb1 = [
                            left_wide[slot * 16 + 4 * sc + ch, :, columns] for sc in range(4)
                        ]
                        real = (ma0 * a0 + mb0 * b0) + (ma1 * a1 + mb1 * b1)
                        imag = (mb0 * a0 - ma0 * b0) + (mb1 * a1 - ma1 * b1)
                        products.append(jnp.concatenate([real, imag], axis=1))
                rows = pl.ds(pl.multiple_of(t * 2 * TILE, 2 * TILE), 2 * TILE)
                return acc + jnp.dot(
                    jnp.concatenate(products, axis=0),
                    table[rows, :],
                    preferred_element_type=jnp.float32,
                )

            lagged = lax.fori_loop(
                0, TILES, tile, jnp.zeros((OWNERS * CH * 16, LAGS), jnp.float32), unroll=2
            )
            for i, slot in enumerate(slots):
                at = g * (NZ * NY) + (2 * q + slot // NY) * NY + slot % NY
                least = jnp.minimum(counts[0, at], counts[1, at])
                for ch in range(CH):
                    factor = jnp.where(least > ch, 1.0, 0.0).astype(jnp.float32)
                    first = (i * CH + ch) * 16
                    pieces[e, slot, ch] = (
                        lagged[first : first + 16] * (1.0 - both * factor)
                    ).astype(jnp.bfloat16)
            for i, slot in enumerate(slots):

                @pl.when(slot != me)
                def _():
                    out_copy(e, slot, slot).start()

            return inner

        lax.fori_loop(0, PEERS // OWNERS, owners, 0)
        return carry

    lax.fori_loop(0, 2, half, 0)

    def store(e):
        return pltpu.make_async_copy(
            result.at[:, :, pl.ds(pl.multiple_of(e * 64, 64), 64), :],
            out_ref.at[:, :, pl.ds(pl.multiple_of(e * 64, 64), 64), :],
            local_sem.at[3 + e],
        )

    for turn in range(2):
        e = (q // 2 + turn) % 2
        for n in range(PEERS - 1):
            out_arrival(e, (me + 1 + n) % PEERS).wait_recv()
        landed[e, me] = pieces[e, me]

        def assemble(n, carry, e=e):
            side = n // CH
            ch = n % CH
            for k in range(ROUNDS):
                parts = []
                for column in range(NY):
                    source = jnp.where(flip[k], NY - 1 - column, column)
                    tile = landed[e, side * NY + source, ch].astype(jnp.float32)
                    parts.append(tile[8 * k : 8 * k + 8])
                for zz in range(2):
                    rows = jnp.concatenate([p[4 * zz : 4 * zz + 4] for p in parts], axis=0)
                    at = pl.multiple_of((side + 4 * e + 2 * zz) * 16, 16)
                    result[k, ch, pl.ds(at, 16), :] = rows.astype(jnp.bfloat16)
            return carry

        lax.fori_loop(0, 2 * CH, assemble, 0)
        store(e).start()

    for n in range(PEERS - 1):
        left_copy(white, me, facing, n).wait_send()
        for e in range(2):
            out_copy(e, (me + 1 + n) % PEERS, facing).wait_send()
    @pl.when(feeds)
    def _():
        feed_copy().wait_send()

    for other in range(4):

        @pl.when(jnp.logical_not(feeds))
        def _():
            ahead_copy(other, other).wait_send()

        @pl.when(spreads)
        def _():
            spread_copy(other).wait_send()

        @pl.when(core == 0)
        def _():
            own_copy(other, other).wait_send()

        @pl.when(core == 1)
        def _():
            mate_copy(other, other).wait_send()

    store(0).wait()
    store(1).wait()


def local(spectra, counts, table):
    bf16 = jnp.bfloat16
    dma = pltpu.SemaphoreType.DMA
    return pl.pallas_call(
        kernel,
        out_shape=jax.ShapeDtypeStruct((ROUNDS, CH, NZ * NY * CH, LAGS), bf16),
        in_specs=[pl.BlockSpec(memory_space=pl.ANY)] * 3,
        out_specs=pl.BlockSpec(memory_space=pl.ANY),
        scratch_shapes=[
            pltpu.VMEM((CH, 2, 2, BINS), jnp.float32),
            pltpu.SMEM(counts.shape, jnp.int32),
            pltpu.VMEM((16, BINS), bf16),
            pltpu.VMEM((16, BINS), bf16),
            pltpu.VMEM((16, BINS), jnp.float32),
            pltpu.VMEM((PEERS, 16, BINS), bf16),
            pltpu.VMEM((PEERS * 16, 16, BINS), bf16),
            pltpu.VMEM((ROUNDS, 4, 16, BINS), bf16),
            pltpu.VMEM((4, 16, BINS), bf16),
            pltpu.VMEM((2 * BINS, LAGS), bf16),
            pltpu.VMEM((2, PEERS, CH, 16, LAGS), bf16),
            pltpu.VMEM((2, PEERS, CH, 16, LAGS), bf16),
            pltpu.VMEM((ROUNDS, CH, NZ * NY * CH, LAGS), bf16),
            dma((5,)),
            pltpu.SemaphoreType.REGULAR((4,)),
            dma((PEERS - 1,)),
            dma((PEERS,)),
            dma((ROUNDS, 4)),
            dma((4,)),
            dma((2,)),
            dma((4,)),
            dma((4,)),
            dma((2, PEERS)),
            dma((2, PEERS)),
        ],
        compiler_params=pltpu.CompilerParams(
            collective_id=0, has_side_effects=True, vmem_limit_bytes=60 * 1024 * 1024
        ),
        cost_estimate=pl.CostEstimate(
            flops=1100000000, bytes_accessed=1600000, transcendentals=0
        ),
    )(spectra, counts, table)


def solution(mesh):
    table = lag_table()

    def whole(spectra, counts):
        return jax.shard_map(
            local,
            mesh=mesh,
            in_specs=(P(("grp", "dev"), None, None, None), P(), P()),
            out_specs=P(None, ("grp", "dev"), None, None),
            check_vma=False,
        )(spectra, counts, jnp.asarray(table))

    return whole
```

```python
import math

import jax
import jax.numpy as jnp
import ml_dtypes
import numpy as np
from jax import lax
from jax.experimental import pallas as pl
from jax.experimental.pallas import tpu as pltpu
from jax.sharding import PartitionSpec as P

LAGS = 128
ROUNDS = 2
NZ = 8
NY = 4
NG = 16
NX = 4
CH = 4
BINS = 2048
TILE = 512
TILES = BINS // TILE
PEERS = 2 * NY
OWNERS = 4
MESH = pl.DeviceIdType.MESH


def lag_table():
    frequency = np.arange(BINS, dtype=np.int64)
    lag_index = np.arange(LAGS, dtype=np.int64) - LAGS // 2
    turns = np.mod(frequency[:, None] * lag_index[None, :], 2 * BINS)
    angles = turns * (math.pi / BINS)
    table = np.stack([np.cos(angles), -np.sin(angles)], 0) / math.sqrt(BINS)
    table = table.reshape(2, TILES, TILE, LAGS).transpose(1, 0, 2, 3).reshape(2 * BINS, LAGS)
    return table.astype(np.float32).astype(ml_dtypes.bfloat16)


def kernel(
    spectra_ref, counts_hbm, table_ref, out_ref,
    raw, counts, white, fed, wide_f32, left, left_wide, right, partner, table, pieces, landed, result,
    local_sem, reply_sem, left_send, left_recv, right_recv, ahead_send, feed_sem, spread_send, mate_send,
    out_send, out_recv,
):
    g = lax.axis_index("grp")
    d = lax.axis_index("dev")
    z = d // NY
    y = d % NY
    core = g % 2
    x = (g // 2) % NX
    parity = z % 2
    q = z // 2
    me = parity * NY + y
    mate_g = g + 1 - 2 * core

    load_raw = pltpu.make_async_copy(spectra_ref, raw, local_sem.at[0])
    load_raw.start()
    load_counts = pltpu.make_async_copy(counts_hbm, counts, local_sem.at[1])
    load_counts.start()
    load_table = pltpu.make_async_copy(table_ref, table, local_sem.at[2])
    load_table.start()

    def peer(slot):
        return (g, (2 * q + slot // NY) * NY + slot % NY)

    def row(other_q, group):
        return (group, (parity + 2 * other_q) * NY + y)

    late = q >= 2
    beside = q + 1 - 2 * (q % 2)
    mate = (mate_g, d)
    column_to = jnp.where(x == NX - 1, NY - 1 - y, y)
    column_from = jnp.where(x == 0, NY - 1 - y, y)

    def ahead(other_q):
        return ((g + 2) % NG, (parity + 2 * other_q) * NY + column_to)

    feeds = jnp.logical_and(x == NX - 1, core == 0)
    spreads = jnp.logical_and(x == 0, core == 0)
    fed_by = ((g + 6) % NG, d)
    feed_to = ((g + 10) % NG, d)

    def behind(other_q):
        spread = jnp.logical_and(spreads, other_q // 2 != q // 2)
        group = jnp.where(spread, g + 8, g - 2 + NG) % NG
        return (group, (parity + 2 * other_q) * NY + column_from)

    barrier = pltpu.get_barrier_semaphore()

    def greet(device, semaphore=barrier):
        pl.semaphore_signal(semaphore, inc=1, device_id=device, device_id_type=MESH)

    @pl.when(jnp.logical_not(late))
    def _():
        for other in (2, 3):
            greet(behind(other))
            greet(row(other, mate_g))

        @pl.when(jnp.logical_not(feeds))
        def _():
            for other in (2, 3):
                greet(ahead(other))

    @pl.when(spreads)
    def _():
        greet(fed_by)

    greet(behind(q))
    greet(behind(beside))
    greet(mate)
    greet(row(beside, mate_g))
    for step in range(1, PEERS):
        greet(peer((me + step) % PEERS))
    near = 4 + PEERS - 1 + jnp.where(feeds, 1, 0)

    load_counts.wait()
    load_raw.wait()
    block = g * (NZ * NY) + d
    for ch in range(CH):
        for s in range(2):
            values = raw[ch, s]
            square = values * values
            lanes = square[:, 0:128]
            for t in range(1, BINS // 128):
                lanes = lanes + square[:, t * 128 : (t + 1) * 128]
            total = jnp.sum(jnp.sum(lanes, axis=0, keepdims=True), axis=1, keepdims=True)
            live = jnp.where(counts[s, block] > ch, 1.0, 0.0).astype(jnp.float32)
            scale = live / jnp.sqrt(total * (1.0 / (2 * BINS)) + 1e-06)
            wide_f32[s * 8 + ch : s * 8 + ch + 1, :] = values[0:1] * scale
            wide_f32[s * 8 + 4 + ch : s * 8 + 4 + ch + 1, :] = values[1:2] * scale
    white[...] = wide_f32[...].astype(jnp.bfloat16)

    @pl.when(jnp.logical_not(late))
    def _():
        pl.semaphore_wait(barrier, near)

    @pl.when(late)
    def _():
        pl.semaphore_wait(barrier, near + 6 - jnp.where(feeds, 2, 0))
        for other in (0, 1):
            greet(behind(other), reply_sem.at[q])
            greet(row(other, mate_g), reply_sem.at[q])

    def ahead_copy(n, other):
        return pltpu.make_async_remote_copy(
            src_ref=white, dst_ref=right.at[1, q],
            send_sem=ahead_send.at[n], recv_sem=right_recv.at[1, q],
            device_id=ahead(other), device_id_type=MESH,
        )

    def own_copy(n, other):
        return pltpu.make_async_remote_copy(
            src_ref=white, dst_ref=right.at[0, q],
            send_sem=mate_send.at[n], recv_sem=right_recv.at[0, q],
            device_id=row(other, mate_g), device_id_type=MESH,
        )

    def mate_copy(n, other):
        return pltpu.make_async_remote_copy(
            src_ref=right.at[1, other], dst_ref=right.at[0, other],
            send_sem=mate_send.at[n], recv_sem=right_recv.at[0, other],
            device_id=mate, device_id_type=MESH,
        )

    def arrival(k, other):
        return pltpu.make_async_remote_copy(
            src_ref=white, dst_ref=right.at[k, other],
            send_sem=ahead_send.at[0], recv_sem=right_recv.at[k, other],
            device_id=mate, device_id_type=MESH,
        )

    facing = (PEERS // 2 + me) % PEERS

    def left_copy(source, slot, target, n):
        return pltpu.make_async_remote_copy(
            src_ref=source, dst_ref=left.at[slot],
            send_sem=left_send.at[n], recv_sem=left_recv.at[slot],
            device_id=peer(target), device_id_type=MESH,
        )

    def in_row(n):
        flipped = y + 1 - 2 * (y % 2)
        return parity * NY + (flipped if n == 1 else (y + 2) % NY if n == 2 else (flipped + 2) % NY)

    def feed_copy():
        return pltpu.make_async_remote_copy(
            src_ref=white, dst_ref=fed, send_sem=feed_sem.at[0], recv_sem=feed_sem.at[1],
            device_id=feed_to, device_id_type=MESH,
        )

    def spread_copy(other):
        return pltpu.make_async_remote_copy(
            src_ref=fed, dst_ref=right.at[1, q],
            send_sem=spread_send.at[other], recv_sem=right_recv.at[1, q],
            device_id=behind(other), device_id_type=MESH,
        )

    def straight(other):
        return jnp.logical_or(jnp.logical_not(feeds), other // 2 == q // 2)

    def send_row(other):
        @pl.when(straight(other))
        def _():
            ahead_copy(other, other).start()

        @pl.when(core == 0)
        def _():
            own_copy(other, other).start()

    @pl.when(feeds)
    def _():
        feed_copy().start()

    @pl.when(late)
    def _():
        for other in (0, 1):
            send_row(other)

    send_row(q)
    send_row(beside)
    for n in range(1, NY):
        left_copy(white, me, in_row(n), n).start()
    left_copy(white, me, facing, 0).start()

    def left_arrival(slot):
        left_copy(white, slot, facing, 0).wait_recv()

    @pl.when(spreads)
    def _():
        feed_copy().wait_recv()

        @pl.when(late)
        def _():
            spread_copy(0).start()
            spread_copy(1).start()

    for n in range(1, NY):
        left_arrival(in_row(n))
        left_copy(left.at[in_row(n)], in_row(n), facing, NY - 1 + n).start()

    for other in (q, beside):
        arrival(1, other).wait_recv()

        @pl.when(core == 1)
        def _():
            mate_copy(other, other).start()

    @pl.when(jnp.logical_not(late))
    def _():
        for other in (2, 3):
            pl.semaphore_wait(
                reply_sem.at[other], 2 + jnp.where(spreads, 1, 0) - jnp.where(feeds, 1, 0)
            )
            send_row(other)

            @pl.when(spreads)
            def _():
                spread_copy(other).start()

    def widen(n, carry):
        row_first = jnp.where(n < NY, parity, 1 - parity) * NY
        slot = row_first + (y + n) % NY

        @pl.when(n >= NY)
        def _():
            left_arrival(slot)

        @pl.when(n > 0)
        def _():
            wide_f32[...] = left[slot].astype(jnp.float32)

        def tile(t, inner):
            columns = pl.ds(pl.multiple_of(t * TILE, TILE), TILE)
            for r in range(16):
                left_wide[slot * 16 + r, :, columns] = jnp.broadcast_to(
                    wide_f32[r : r + 1, columns], (16, TILE)
                ).astype(jnp.bfloat16)
            return inner

        lax.fori_loop(0, TILES, tile, 0)
        return carry

    lax.fori_loop(0, PEERS, widen, 0)
    load_table.wait()

    mirror = x == 0
    flip = [jnp.logical_and(mirror, core == 0), mirror]
    row_id = lax.broadcasted_iota(jnp.int32, (16, LAGS), 0)

    def out_copy(e, n, slot):
        return pltpu.make_async_remote_copy(
            src_ref=pieces.at[e, slot], dst_ref=landed.at[e, me],
            send_sem=out_send.at[e, n], recv_sem=out_recv.at[e, me],
            device_id=peer(slot), device_id_type=MESH,
        )

    def out_arrival(e, slot):
        return pltpu.make_async_remote_copy(
            src_ref=pieces.at[e, slot], dst_ref=landed.at[e, slot],
            send_sem=out_send.at[e, 0], recv_sem=out_recv.at[e, slot],
            device_id=peer(slot), device_id_type=MESH,
        )

    def half(turn, carry):
        e = (q // 2 + turn) % 2
        @pl.when(turn == 1)
        def _():
            for zz in range(2):
                arrival(1, 2 * e + zz).wait_recv()

                @pl.when(core == 1)
                def _():
                    mate_copy(2 * e + zz, 2 * e + zz).start()

        for zz in range(2):
            arrival(0, 2 * e + zz).wait_recv()

        def gather(t, inner):
            columns = pl.ds(pl.multiple_of(t * TILE, TILE), TILE)
            parts = [
                right[k, 2 * e + zz, :, columns].astype(jnp.float32)
                for k in range(ROUNDS)
                for zz in range(2)
            ]
            for sc in range(4):
                rows = jnp.concatenate([p[4 * sc : 4 * sc + 4] for p in parts], axis=0)
                partner[sc, :, columns] = rows.astype(jnp.bfloat16)
            return inner

        lax.fori_loop(0, TILES, gather, 0)

        limit = jnp.zeros((16, LAGS), jnp.int32)
        for k in range(ROUNDS):
            column = jnp.where(flip[k], NY - 1 - y, y)
            for zz in range(2):
                group = (g - 1 - k + NG) % NG
                at = group * (NZ * NY) + (parity + 2 * (2 * e + zz)) * NY + column
                least = jnp.minimum(counts[0, at], counts[1, at])
                limit = jnp.where(row_id // 4 == k * 2 + zz, least, limit)
        both = jnp.where(row_id % 4 < limit, 0.5, 0.0).astype(jnp.float32)

        def owners(n, inner):
            pair = (y // 2 + 1 + n) % 2
            slots = [(i // 2) * NY + pair * 2 + i % 2 for i in range(OWNERS)]

            def tile(t, acc):
                columns = pl.ds(pl.multiple_of(t * TILE, TILE), TILE)
                a0, b0, a1, b1 = [partner[sc, :, columns] for sc in range(4)]
                products = []
                for slot in slots:
                    for ch in range(CH):
                        ma0, mb0, ma1, mb1 = [
                            left_wide[slot * 16 + 4 * sc + ch, :, columns] for sc in range(4)
                        ]
                        real = (ma0 * a0 + mb0 * b0) + (ma1 * a1 + mb1 * b1)
                        imag = (mb0 * a0 - ma0 * b0) + (mb1 * a1 - ma1 * b1)
                        products.append(jnp.concatenate([real, imag], axis=1))
                rows = pl.ds(pl.multiple_of(t * 2 * TILE, 2 * TILE), 2 * TILE)
                return acc + jnp.dot(
                    jnp.concatenate(products, axis=0),
                    table[rows, :],
                    preferred_element_type=jnp.float32,
                )

            lagged = lax.fori_loop(
                0, TILES, tile, jnp.zeros((OWNERS * CH * 16, LAGS), jnp.float32), unroll=2
            )
            for i, slot in enumerate(slots):
                at = g * (NZ * NY) + (2 * q + slot // NY) * NY + slot % NY
                least = jnp.minimum(counts[0, at], counts[1, at])
                for ch in range(CH):
                    factor = jnp.where(least > ch, 1.0, 0.0).astype(jnp.float32)
                    first = (i * CH + ch) * 16
                    pieces[e, slot, ch] = (
                        lagged[first : first + 16] * (1.0 - both * factor)
                    ).astype(jnp.bfloat16)
            for i, slot in enumerate(slots):

                @pl.when(slot != me)
                def _():
                    out_copy(e, slot, slot).start()

            return inner

        lax.fori_loop(0, PEERS // OWNERS, owners, 0)
        return carry

    lax.fori_loop(0, 2, half, 0)

    def store(e):
        return pltpu.make_async_copy(
            result.at[:, :, pl.ds(pl.multiple_of(e * 64, 64), 64), :],
            out_ref.at[:, :, pl.ds(pl.multiple_of(e * 64, 64), 64), :],
            local_sem.at[3 + e],
        )

    for turn in range(2):
        e = (q // 2 + turn) % 2
        for n in range(PEERS - 1):
            out_arrival(e, (me + 1 + n) % PEERS).wait_recv()
        landed[e, me] = pieces[e, me]

        def assemble(n, carry, e=e):
            side = n // CH
            ch = n % CH
            for k in range(ROUNDS):
                parts = []
                for column in range(NY):
                    source = jnp.where(flip[k], NY - 1 - column, column)
                    tile = landed[e, side * NY + source, ch].astype(jnp.float32)
                    parts.append(tile[8 * k : 8 * k + 8])
                for zz in range(2):
                    rows = jnp.concatenate([p[4 * zz : 4 * zz + 4] for p in parts], axis=0)
                    at = pl.multiple_of((side + 4 * e + 2 * zz) * 16, 16)
                    result[k, ch, pl.ds(at, 16), :] = rows.astype(jnp.bfloat16)
            return carry

        lax.fori_loop(0, 2 * CH, assemble, 0)
        store(e).start()

    for n in range(PEERS - 1):
        left_copy(white, me, facing, n).wait_send()
        for e in range(2):
            out_copy(e, (me + 1 + n) % PEERS, facing).wait_send()
    @pl.when(feeds)
    def _():
        feed_copy().wait_send()

    for other in range(4):

        @pl.when(straight(other))
        def _():
            ahead_copy(other, other).wait_send()

        @pl.when(jnp.logical_and(spreads, other // 2 != q // 2))
        def _():
            spread_copy(other).wait_send()

        @pl.when(core == 0)
        def _():
            own_copy(other, other).wait_send()

        @pl.when(core == 1)
        def _():
            mate_copy(other, other).wait_send()

    store(0).wait()
    store(1).wait()


def local(spectra, counts, table):
    bf16 = jnp.bfloat16
    dma = pltpu.SemaphoreType.DMA
    return pl.pallas_call(
        kernel,
        out_shape=jax.ShapeDtypeStruct((ROUNDS, CH, NZ * NY * CH, LAGS), bf16),
        in_specs=[pl.BlockSpec(memory_space=pl.ANY)] * 3,
        out_specs=pl.BlockSpec(memory_space=pl.ANY),
        scratch_shapes=[
            pltpu.VMEM((CH, 2, 2, BINS), jnp.float32),
            pltpu.SMEM(counts.shape, jnp.int32),
            pltpu.VMEM((16, BINS), bf16),
            pltpu.VMEM((16, BINS), bf16),
            pltpu.VMEM((16, BINS), jnp.float32),
            pltpu.VMEM((PEERS, 16, BINS), bf16),
            pltpu.VMEM((PEERS * 16, 16, BINS), bf16),
            pltpu.VMEM((ROUNDS, 4, 16, BINS), bf16),
            pltpu.VMEM((4, 16, BINS), bf16),
            pltpu.VMEM((2 * BINS, LAGS), bf16),
            pltpu.VMEM((2, PEERS, CH, 16, LAGS), bf16),
            pltpu.VMEM((2, PEERS, CH, 16, LAGS), bf16),
            pltpu.VMEM((ROUNDS, CH, NZ * NY * CH, LAGS), bf16),
            dma((5,)),
            pltpu.SemaphoreType.REGULAR((4,)),
            dma((PEERS - 1,)),
            dma((PEERS,)),
            dma((ROUNDS, 4)),
            dma((4,)),
            dma((2,)),
            dma((4,)),
            dma((4,)),
            dma((2, PEERS)),
            dma((2, PEERS)),
        ],
        compiler_params=pltpu.CompilerParams(
            collective_id=0, has_side_effects=True, vmem_limit_bytes=60 * 1024 * 1024
        ),
        cost_estimate=pl.CostEstimate(
            flops=1100000000, bytes_accessed=1600000, transcendentals=0
        ),
    )(spectra, counts, table)


def solution(mesh):
    table = lag_table()

    def whole(spectra, counts):
        return jax.shard_map(
            local,
            mesh=mesh,
            in_specs=(P(("grp", "dev"), None, None, None), P(), P()),
            out_specs=P(None, ("grp", "dev"), None, None),
            check_vma=False,
        )(spectra, counts, jnp.asarray(table))

    return whole
```

```python
import math

import jax
import jax.numpy as jnp
import ml_dtypes
import numpy as np
from jax import lax
from jax.experimental import pallas as pl
from jax.experimental.pallas import tpu as pltpu
from jax.sharding import PartitionSpec as P

LAGS = 128
ROUNDS = 2
NZ = 8
NY = 4
NG = 16
NX = 4
CH = 4
BINS = 2048
TILE = 512
TILES = BINS // TILE
PEERS = 2 * NY
OWNERS = 4
MESH = pl.DeviceIdType.MESH


def lag_table():
    frequency = np.arange(BINS, dtype=np.int64)
    lag_index = np.arange(LAGS, dtype=np.int64) - LAGS // 2
    turns = np.mod(frequency[:, None] * lag_index[None, :], 2 * BINS)
    angles = turns * (math.pi / BINS)
    table = np.stack([np.cos(angles), -np.sin(angles)], 0) / math.sqrt(BINS)
    table = table.reshape(2, TILES, TILE, LAGS).transpose(1, 0, 2, 3).reshape(2 * BINS, LAGS)
    return table.astype(np.float32).astype(ml_dtypes.bfloat16)


def kernel(
    spectra_ref, counts_hbm, table_ref, out_ref,
    raw, counts, white, fed, wide_f32, left, left_wide, right, partner, table, pieces, landed, result,
    local_sem, reply_sem, left_send, left_recv, right_recv, ahead_send, feed_sem, spread_send, mate_send,
    out_send, out_recv,
):
    g = lax.axis_index("grp")
    d = lax.axis_index("dev")
    z = d // NY
    y = d % NY
    core = g % 2
    x = (g // 2) % NX
    parity = z % 2
    q = z // 2
    me = parity * NY + y
    mate_g = g + 1 - 2 * core

    load_raw = pltpu.make_async_copy(spectra_ref, raw, local_sem.at[0])
    load_raw.start()
    load_counts = pltpu.make_async_copy(counts_hbm, counts, local_sem.at[1])
    load_counts.start()
    load_table = pltpu.make_async_copy(table_ref, table, local_sem.at[2])
    load_table.start()

    def peer(slot):
        return (g, (2 * q + slot // NY) * NY + slot % NY)

    def row(other_q, group):
        return (group, (parity + 2 * other_q) * NY + y)

    late = q >= 2
    beside = q + 1 - 2 * (q % 2)
    mate = (mate_g, d)
    column_to = jnp.where(x == NX - 1, NY - 1 - y, y)
    column_from = jnp.where(x == 0, NY - 1 - y, y)

    def ahead(other_q):
        return ((g + 2) % NG, (parity + 2 * other_q) * NY + column_to)

    feeds = jnp.logical_and(x == NX - 1, core == 0)
    spreads = jnp.logical_and(x == 0, core == 0)
    fed_by = ((g + 6) % NG, d)
    feed_to = ((g + 10) % NG, d)

    def behind(other_q):
        spread = jnp.logical_and(spreads, other_q // 2 != q // 2)
        group = jnp.where(spread, g + 8, g - 2 + NG) % NG
        return (group, (parity + 2 * other_q) * NY + column_from)

    barrier = pltpu.get_barrier_semaphore()

    def greet(device, semaphore=barrier):
        pl.semaphore_signal(semaphore, inc=1, device_id=device, device_id_type=MESH)

    @pl.when(jnp.logical_not(late))
    def _():
        for other in (2, 3):
            greet(behind(other))
            greet(row(other, mate_g))

        @pl.when(jnp.logical_not(feeds))
        def _():
            for other in (2, 3):
                greet(ahead(other))

    @pl.when(spreads)
    def _():
        greet(fed_by)

    greet(behind(q))
    greet(behind(beside))
    greet(mate)
    greet(row(beside, mate_g))
    for step in range(1, PEERS):
        greet(peer((me + step) % PEERS))
    near = 4 + PEERS - 1 + jnp.where(feeds, 1, 0)

    load_counts.wait()
    load_raw.wait()
    block = g * (NZ * NY) + d
    for ch in range(CH):
        for s in range(2):
            values = raw[ch, s]
            square = values * values
            lanes = square[:, 0:128]
            for t in range(1, BINS // 128):
                lanes = lanes + square[:, t * 128 : (t + 1) * 128]
            total = jnp.sum(jnp.sum(lanes, axis=0, keepdims=True), axis=1, keepdims=True)
            live = jnp.where(counts[s, block] > ch, 1.0, 0.0).astype(jnp.float32)
            scale = live / jnp.sqrt(total * (1.0 / (2 * BINS)) + 1e-06)
            wide_f32[s * 8 + ch : s * 8 + ch + 1, :] = values[0:1] * scale
            wide_f32[s * 8 + 4 + ch : s * 8 + 4 + ch + 1, :] = values[1:2] * scale
    white[...] = wide_f32[...].astype(jnp.bfloat16)

    @pl.when(jnp.logical_not(late))
    def _():
        pl.semaphore_wait(barrier, near)

    @pl.when(late)
    def _():
        pl.semaphore_wait(barrier, near + 6 - jnp.where(feeds, 2, 0))
        for other in (0, 1):
            greet(behind(other), reply_sem.at[q])
            greet(row(other, mate_g), reply_sem.at[q])

    def ahead_copy(n, other):
        return pltpu.make_async_remote_copy(
            src_ref=white, dst_ref=right.at[1, q],
            send_sem=ahead_send.at[n], recv_sem=right_recv.at[1, q],
            device_id=ahead(other), device_id_type=MESH,
        )

    def own_copy(n, other):
        return pltpu.make_async_remote_copy(
            src_ref=white, dst_ref=right.at[0, q],
            send_sem=mate_send.at[n], recv_sem=right_recv.at[0, q],
            device_id=row(other, mate_g), device_id_type=MESH,
        )

    def mate_copy(n, other):
        return pltpu.make_async_remote_copy(
            src_ref=right.at[1, other], dst_ref=right.at[0, other],
            send_sem=mate_send.at[n], recv_sem=right_recv.at[0, other],
            device_id=mate, device_id_type=MESH,
        )

    def arrival(k, other):
        return pltpu.make_async_remote_copy(
            src_ref=white, dst_ref=right.at[k, other],
            send_sem=ahead_send.at[0], recv_sem=right_recv.at[k, other],
            device_id=mate, device_id_type=MESH,
        )

    facing = (PEERS // 2 + me) % PEERS

    def left_copy(source, slot, target, n):
        return pltpu.make_async_remote_copy(
            src_ref=source, dst_ref=left.at[slot],
            send_sem=left_send.at[n], recv_sem=left_recv.at[slot],
            device_id=peer(target), device_id_type=MESH,
        )

    def in_row(n):
        flipped = y + 1 - 2 * (y % 2)
        return parity * NY + (flipped if n == 1 else (y + 2) % NY if n == 2 else (flipped + 2) % NY)

    def feed_copy():
        return pltpu.make_async_remote_copy(
            src_ref=white, dst_ref=fed, send_sem=feed_sem.at[0], recv_sem=feed_sem.at[1],
            device_id=feed_to, device_id_type=MESH,
        )

    def spread_copy(other):
        return pltpu.make_async_remote_copy(
            src_ref=fed, dst_ref=right.at[1, q],
            send_sem=spread_send.at[other], recv_sem=right_recv.at[1, q],
            device_id=behind(other), device_id_type=MESH,
        )

    def straight(other):
        return jnp.logical_or(jnp.logical_not(feeds), other // 2 == q // 2)

    def send_row(other):
        @pl.when(straight(other))
        def _():
            ahead_copy(other, other).start()

        @pl.when(core == 0)
        def _():
            own_copy(other, other).start()

    @pl.when(feeds)
    def _():
        feed_copy().start()

    @pl.when(late)
    def _():
        for other in (0, 1):
            send_row(other)

    send_row(q)
    send_row(beside)
    for n in range(1, NY):
        left_copy(white, me, in_row(n), n).start()
    left_copy(white, me, facing, 0).start()

    def left_arrival(slot):
        left_copy(white, slot, facing, 0).wait_recv()

    @pl.when(spreads)
    def _():
        feed_copy().wait_recv()

        @pl.when(late)
        def _():
            spread_copy(0).start()
            spread_copy(1).start()

    for n in range(1, NY):
        left_arrival(in_row(n))
        left_copy(left.at[in_row(n)], in_row(n), facing, NY - 1 + n).start()

    for other in (q, beside):
        arrival(1, other).wait_recv()

        @pl.when(core == 1)
        def _():
            mate_copy(other, other).start()

    @pl.when(jnp.logical_not(late))
    def _():
        for other in (2, 3):
            pl.semaphore_wait(
                reply_sem.at[other], 2 + jnp.where(spreads, 1, 0) - jnp.where(feeds, 1, 0)
            )
            send_row(other)

            @pl.when(spreads)
            def _():
                spread_copy(other).start()

    def widen(n, carry):
        row_first = jnp.where(n < NY, parity, 1 - parity) * NY
        slot = row_first + (y + n) % NY

        @pl.when(n >= NY)
        def _():
            left_arrival(slot)

        @pl.when(n > 0)
        def _():
            wide_f32[...] = left[slot].astype(jnp.float32)

        def tile(t, inner):
            columns = pl.ds(pl.multiple_of(t * TILE, TILE), TILE)
            for r in range(16):
                left_wide[slot * 16 + r, :, columns] = jnp.broadcast_to(
                    wide_f32[r : r + 1, columns], (16, TILE)
                ).astype(jnp.bfloat16)
            return inner

        lax.fori_loop(0, TILES, tile, 0)
        return carry

    lax.fori_loop(0, NY, widen, 0)
    load_table.wait()

    mirror = x == 0
    flip = [jnp.logical_and(mirror, core == 0), mirror]
    row_id = lax.broadcasted_iota(jnp.int32, (16, LAGS), 0)

    def out_copy(e, n, slot):
        return pltpu.make_async_remote_copy(
            src_ref=pieces.at[e, slot], dst_ref=landed.at[e, me],
            send_sem=out_send.at[e, n], recv_sem=out_recv.at[e, me],
            device_id=peer(slot), device_id_type=MESH,
        )

    def out_arrival(e, slot):
        return pltpu.make_async_remote_copy(
            src_ref=pieces.at[e, slot], dst_ref=landed.at[e, slot],
            send_sem=out_send.at[e, 0], recv_sem=out_recv.at[e, slot],
            device_id=peer(slot), device_id_type=MESH,
        )

    def half(turn, carry):
        e = (q // 2 + turn) % 2
        @pl.when(turn == 1)
        def _():
            for zz in range(2):
                arrival(1, 2 * e + zz).wait_recv()

                @pl.when(core == 1)
                def _():
                    mate_copy(2 * e + zz, 2 * e + zz).start()

        for zz in range(2):
            arrival(0, 2 * e + zz).wait_recv()

        def gather(t, inner):
            columns = pl.ds(pl.multiple_of(t * TILE, TILE), TILE)
            parts = [
                right[k, 2 * e + zz, :, columns].astype(jnp.float32)
                for k in range(ROUNDS)
                for zz in range(2)
            ]
            for sc in range(4):
                rows = jnp.concatenate([p[4 * sc : 4 * sc + 4] for p in parts], axis=0)
                partner[sc, :, columns] = rows.astype(jnp.bfloat16)
            return inner

        lax.fori_loop(0, TILES, gather, 0)

        limit = jnp.zeros((16, LAGS), jnp.int32)
        for k in range(ROUNDS):
            column = jnp.where(flip[k], NY - 1 - y, y)
            for zz in range(2):
                group = (g - 1 - k + NG) % NG
                at = group * (NZ * NY) + (parity + 2 * (2 * e + zz)) * NY + column
                least = jnp.minimum(counts[0, at], counts[1, at])
                limit = jnp.where(row_id // 4 == k * 2 + zz, least, limit)
        both = jnp.where(row_id % 4 < limit, 0.5, 0.0).astype(jnp.float32)

        def owners(n, inner):
            first = turn == 0
            pair = (y // 2 + 1 + n) % 2
            side = (parity + n) % 2
            slots = [
                jnp.where(first, side * NY + i, (i // 2) * NY + pair * 2 + i % 2)
                for i in range(OWNERS)
            ]

            @pl.when(jnp.logical_and(first, n == 1))
            def _():
                lax.fori_loop(NY, PEERS, widen, 0)


            def tile(t, acc):
                columns = pl.ds(pl.multiple_of(t * TILE, TILE), TILE)
                a0, b0, a1, b1 = [partner[sc, :, columns] for sc in range(4)]
                products = []
                for slot in slots:
                    for ch in range(CH):
                        ma0, mb0, ma1, mb1 = [
                            left_wide[slot * 16 + 4 * sc + ch, :, columns] for sc in range(4)
                        ]
                        real = (ma0 * a0 + mb0 * b0) + (ma1 * a1 + mb1 * b1)
                        imag = (mb0 * a0 - ma0 * b0) + (mb1 * a1 - ma1 * b1)
                        products.append(jnp.concatenate([real, imag], axis=1))
                rows = pl.ds(pl.multiple_of(t * 2 * TILE, 2 * TILE), 2 * TILE)
                return acc + jnp.dot(
                    jnp.concatenate(products, axis=0),
                    table[rows, :],
                    preferred_element_type=jnp.float32,
                )

            lagged = lax.fori_loop(
                0, TILES, tile, jnp.zeros((OWNERS * CH * 16, LAGS), jnp.float32), unroll=2
            )
            for i, slot in enumerate(slots):
                at = g * (NZ * NY) + (2 * q + slot // NY) * NY + slot % NY
                least = jnp.minimum(counts[0, at], counts[1, at])
                for ch in range(CH):
                    factor = jnp.where(least > ch, 1.0, 0.0).astype(jnp.float32)
                    at_row = (i * CH + ch) * 16
                    pieces[e, slot, ch] = (
                        lagged[at_row : at_row + 16] * (1.0 - both * factor)
                    ).astype(jnp.bfloat16)
            for i, slot in enumerate(slots):

                @pl.when(slot != me)
                def _():
                    out_copy(e, slot, slot).start()

            return inner

        lax.fori_loop(0, PEERS // OWNERS, owners, 0)
        return carry

    lax.fori_loop(0, 2, half, 0)

    def store(e):
        return pltpu.make_async_copy(
            result.at[:, :, pl.ds(pl.multiple_of(e * 64, 64), 64), :],
            out_ref.at[:, :, pl.ds(pl.multiple_of(e * 64, 64), 64), :],
            local_sem.at[3 + e],
        )

    for turn in range(2):
        e = (q // 2 + turn) % 2
        for n in range(PEERS - 1):
            out_arrival(e, (me + 1 + n) % PEERS).wait_recv()
        landed[e, me] = pieces[e, me]

        def assemble(n, carry, e=e):
            side = n // CH
            ch = n % CH
            for k in range(ROUNDS):
                parts = []
                for column in range(NY):
                    source = jnp.where(flip[k], NY - 1 - column, column)
                    tile = landed[e, side * NY + source, ch].astype(jnp.float32)
                    parts.append(tile[8 * k : 8 * k + 8])
                for zz in range(2):
                    rows = jnp.concatenate([p[4 * zz : 4 * zz + 4] for p in parts], axis=0)
                    at = pl.multiple_of((side + 4 * e + 2 * zz) * 16, 16)
                    result[k, ch, pl.ds(at, 16), :] = rows.astype(jnp.bfloat16)
            return carry

        lax.fori_loop(0, 2 * CH, assemble, 0)
        store(e).start()

    for n in range(PEERS - 1):
        left_copy(white, me, facing, n).wait_send()
        for e in range(2):
            out_copy(e, (me + 1 + n) % PEERS, facing).wait_send()
    @pl.when(feeds)
    def _():
        feed_copy().wait_send()

    for other in range(4):

        @pl.when(straight(other))
        def _():
            ahead_copy(other, other).wait_send()

        @pl.when(jnp.logical_and(spreads, other // 2 != q // 2))
        def _():
            spread_copy(other).wait_send()

        @pl.when(core == 0)
        def _():
            own_copy(other, other).wait_send()

        @pl.when(core == 1)
        def _():
            mate_copy(other, other).wait_send()

    store(0).wait()
    store(1).wait()


def local(spectra, counts, table):
    bf16 = jnp.bfloat16
    dma = pltpu.SemaphoreType.DMA
    return pl.pallas_call(
        kernel,
        out_shape=jax.ShapeDtypeStruct((ROUNDS, CH, NZ * NY * CH, LAGS), bf16),
        in_specs=[pl.BlockSpec(memory_space=pl.ANY)] * 3,
        out_specs=pl.BlockSpec(memory_space=pl.ANY),
        scratch_shapes=[
            pltpu.VMEM((CH, 2, 2, BINS), jnp.float32),
            pltpu.SMEM(counts.shape, jnp.int32),
            pltpu.VMEM((16, BINS), bf16),
            pltpu.VMEM((16, BINS), bf16),
            pltpu.VMEM((16, BINS), jnp.float32),
            pltpu.VMEM((PEERS, 16, BINS), bf16),
            pltpu.VMEM((PEERS * 16, 16, BINS), bf16),
            pltpu.VMEM((ROUNDS, 4, 16, BINS), bf16),
            pltpu.VMEM((4, 16, BINS), bf16),
            pltpu.VMEM((2 * BINS, LAGS), bf16),
            pltpu.VMEM((2, PEERS, CH, 16, LAGS), bf16),
            pltpu.VMEM((2, PEERS, CH, 16, LAGS), bf16),
            pltpu.VMEM((ROUNDS, CH, NZ * NY * CH, LAGS), bf16),
            dma((5,)),
            pltpu.SemaphoreType.REGULAR((4,)),
            dma((PEERS - 1,)),
            dma((PEERS,)),
            dma((ROUNDS, 4)),
            dma((4,)),
            dma((2,)),
            dma((4,)),
            dma((4,)),
            dma((2, PEERS)),
            dma((2, PEERS)),
        ],
        compiler_params=pltpu.CompilerParams(
            collective_id=0, has_side_effects=True, vmem_limit_bytes=60 * 1024 * 1024
        ),
        cost_estimate=pl.CostEstimate(
            flops=1100000000, bytes_accessed=1600000, transcendentals=0
        ),
    )(spectra, counts, table)


def solution(mesh):
    table = lag_table()

    def whole(spectra, counts):
        return jax.shard_map(
            local,
            mesh=mesh,
            in_specs=(P(("grp", "dev"), None, None, None), P(), P()),
            out_specs=P(None, ("grp", "dev"), None, None),
            check_vma=False,
        )(spectra, counts, jnp.asarray(table))

    return whole
```

```python
import math

import jax
import jax.numpy as jnp
import ml_dtypes
import numpy as np
from jax import lax
from jax.experimental import pallas as pl
from jax.experimental.pallas import tpu as pltpu
from jax.sharding import PartitionSpec as P

LAGS = 128
ROUNDS = 2
NZ = 8
NY = 4
NG = 16
NX = 4
CH = 4
BINS = 2048
TILE = 512
TILES = BINS // TILE
PEERS = 2 * NY
OWNERS = 4
MESH = pl.DeviceIdType.MESH


def lag_table():
    frequency = np.arange(BINS, dtype=np.int64)
    lag_index = np.arange(LAGS, dtype=np.int64) - LAGS // 2
    turns = np.mod(frequency[:, None] * lag_index[None, :], 2 * BINS)
    angles = turns * (math.pi / BINS)
    table = np.stack([np.cos(angles), -np.sin(angles)], 0) / math.sqrt(BINS)
    table = table.reshape(2, TILES, TILE, LAGS).transpose(1, 0, 2, 3).reshape(2 * BINS, LAGS)
    return table.astype(np.float32).astype(ml_dtypes.bfloat16)


def kernel(
    spectra_ref, counts_hbm, table_ref, out_ref,
    raw, counts, white, fed, wide_f32, left, left_wide, right, partner, table, pieces, landed, result,
    local_sem, reply_sem, left_send, left_recv, right_recv, ahead_send, feed_sem, spread_send, mate_send,
    out_send, out_recv,
):
    g = lax.axis_index("grp")
    d = lax.axis_index("dev")
    z = d // NY
    y = d % NY
    core = g % 2
    x = (g // 2) % NX
    parity = z % 2
    q = z // 2
    me = parity * NY + y
    mate_g = g + 1 - 2 * core

    load_raw = pltpu.make_async_copy(spectra_ref, raw, local_sem.at[0])
    load_raw.start()
    load_counts = pltpu.make_async_copy(counts_hbm, counts, local_sem.at[1])
    load_counts.start()
    load_table = pltpu.make_async_copy(table_ref, table, local_sem.at[2])
    load_table.start()

    def peer(slot):
        return (g, (2 * q + slot // NY) * NY + slot % NY)

    def row(other_q, group):
        return (group, (parity + 2 * other_q) * NY + y)

    late = q >= 2
    beside = q + 1 - 2 * (q % 2)
    mate = (mate_g, d)
    column_to = jnp.where(x == NX - 1, NY - 1 - y, y)
    column_from = jnp.where(x == 0, NY - 1 - y, y)

    def ahead(other_q):
        return ((g + 2) % NG, (parity + 2 * other_q) * NY + column_to)

    feeds = jnp.logical_and(x == NX - 1, core == 0)
    spreads = jnp.logical_and(x == 0, core == 0)
    fed_by = ((g + 6) % NG, d)
    feed_to = ((g + 10) % NG, d)

    def behind(other_q):
        spread = jnp.logical_and(spreads, other_q // 2 != q // 2)
        group = jnp.where(spread, g + 8, g - 2 + NG) % NG
        return (group, (parity + 2 * other_q) * NY + column_from)

    barrier = pltpu.get_barrier_semaphore()

    def greet(device, semaphore=barrier):
        pl.semaphore_signal(semaphore, inc=1, device_id=device, device_id_type=MESH)

    @pl.when(jnp.logical_not(late))
    def _():
        for other in (2, 3):
            greet(behind(other))
            greet(row(other, mate_g))

        @pl.when(jnp.logical_not(feeds))
        def _():
            for other in (2, 3):
                greet(ahead(other))

    @pl.when(spreads)
    def _():
        greet(fed_by)

    greet(behind(q))
    greet(behind(beside))
    greet(mate)
    greet(row(beside, mate_g))
    for step in range(1, PEERS):
        greet(peer((me + step) % PEERS))
    near = 4 + PEERS - 1 + jnp.where(feeds, 1, 0)

    load_counts.wait()
    load_raw.wait()
    block = g * (NZ * NY) + d
    for ch in range(CH):
        for s in range(2):
            values = raw[ch, s]
            square = values * values
            lanes = square[:, 0:128]
            for t in range(1, BINS // 128):
                lanes = lanes + square[:, t * 128 : (t + 1) * 128]
            total = jnp.sum(jnp.sum(lanes, axis=0, keepdims=True), axis=1, keepdims=True)
            live = jnp.where(counts[s, block] > ch, 1.0, 0.0).astype(jnp.float32)
            scale = live / jnp.sqrt(total * (1.0 / (2 * BINS)) + 1e-06)
            wide_f32[s * 8 + ch : s * 8 + ch + 1, :] = values[0:1] * scale
            wide_f32[s * 8 + 4 + ch : s * 8 + 4 + ch + 1, :] = values[1:2] * scale
    white[...] = wide_f32[...].astype(jnp.bfloat16)

    @pl.when(jnp.logical_not(late))
    def _():
        pl.semaphore_wait(barrier, near)

    @pl.when(late)
    def _():
        pl.semaphore_wait(barrier, near + 6 - jnp.where(feeds, 2, 0))
        for other in (0, 1):
            greet(behind(other), reply_sem.at[q])
            greet(row(other, mate_g), reply_sem.at[q])

    def ahead_copy(n, other):
        return pltpu.make_async_remote_copy(
            src_ref=white, dst_ref=right.at[1, q],
            send_sem=ahead_send.at[n], recv_sem=right_recv.at[1, q],
            device_id=ahead(other), device_id_type=MESH,
        )

    def own_copy(n, other):
        return pltpu.make_async_remote_copy(
            src_ref=white, dst_ref=right.at[0, q],
            send_sem=mate_send.at[n], recv_sem=right_recv.at[0, q],
            device_id=row(other, mate_g), device_id_type=MESH,
        )

    def mate_copy(n, other):
        return pltpu.make_async_remote_copy(
            src_ref=right.at[1, other], dst_ref=right.at[0, other],
            send_sem=mate_send.at[n], recv_sem=right_recv.at[0, other],
            device_id=mate, device_id_type=MESH,
        )

    def arrival(k, other):
        return pltpu.make_async_remote_copy(
            src_ref=white, dst_ref=right.at[k, other],
            send_sem=ahead_send.at[0], recv_sem=right_recv.at[k, other],
            device_id=mate, device_id_type=MESH,
        )

    facing = (PEERS // 2 + me) % PEERS

    def left_copy(source, slot, target, n):
        return pltpu.make_async_remote_copy(
            src_ref=source, dst_ref=left.at[slot],
            send_sem=left_send.at[n], recv_sem=left_recv.at[slot],
            device_id=peer(target), device_id_type=MESH,
        )

    def in_row(n):
        flipped = y + 1 - 2 * (y % 2)
        return parity * NY + (flipped if n == 1 else (y + 2) % NY if n == 2 else (flipped + 2) % NY)

    def feed_copy():
        return pltpu.make_async_remote_copy(
            src_ref=white, dst_ref=fed, send_sem=feed_sem.at[0], recv_sem=feed_sem.at[1],
            device_id=feed_to, device_id_type=MESH,
        )

    def spread_copy(other):
        return pltpu.make_async_remote_copy(
            src_ref=fed, dst_ref=right.at[1, q],
            send_sem=spread_send.at[other], recv_sem=right_recv.at[1, q],
            device_id=behind(other), device_id_type=MESH,
        )

    def straight(other):
        return jnp.logical_or(jnp.logical_not(feeds), other // 2 == q // 2)

    def send_row(other):
        @pl.when(straight(other))
        def _():
            ahead_copy(other, other).start()

        @pl.when(core == 0)
        def _():
            own_copy(other, other).start()

    @pl.when(feeds)
    def _():
        feed_copy().start()

    @pl.when(late)
    def _():
        for other in (0, 1):
            send_row(other)

    send_row(q)
    send_row(beside)
    for n in range(1, NY):
        left_copy(white, me, in_row(n), n).start()
    left_copy(white, me, facing, 0).start()

    def left_arrival(slot):
        left_copy(white, slot, facing, 0).wait_recv()

    @pl.when(jnp.logical_and(spreads, late))
    def _():
        feed_copy().wait_recv()
        spread_copy(0).start()
        spread_copy(1).start()

    for n in range(1, NY):
        left_arrival(in_row(n))
        left_copy(left.at[in_row(n)], in_row(n), facing, NY - 1 + n).start()

    @pl.when(jnp.logical_not(late))
    def _():
        @pl.when(spreads)
        def _():
            feed_copy().wait_recv()

        for other in (2, 3):
            pl.semaphore_wait(
                reply_sem.at[other], 2 + jnp.where(spreads, 1, 0) - jnp.where(feeds, 1, 0)
            )
            send_row(other)

            @pl.when(spreads)
            def _():
                spread_copy(other).start()

    for other in (q, beside):
        arrival(1, other).wait_recv()

        @pl.when(core == 1)
        def _():
            mate_copy(other, other).start()

    def widen(n, carry):
        row_first = jnp.where(n < NY, parity, 1 - parity) * NY
        slot = row_first + (y + n) % NY

        @pl.when(n >= NY)
        def _():
            left_arrival(slot)

        @pl.when(n > 0)
        def _():
            wide_f32[...] = left[slot].astype(jnp.float32)

        def tile(t, inner):
            columns = pl.ds(pl.multiple_of(t * TILE, TILE), TILE)
            for r in range(16):
                left_wide[slot * 16 + r, :, columns] = jnp.broadcast_to(
                    wide_f32[r : r + 1, columns], (16, TILE)
                ).astype(jnp.bfloat16)
            return inner

        lax.fori_loop(0, TILES, tile, 0)
        return carry

    lax.fori_loop(0, NY, widen, 0)
    load_table.wait()

    mirror = x == 0
    flip = [jnp.logical_and(mirror, core == 0), mirror]
    row_id = lax.broadcasted_iota(jnp.int32, (16, LAGS), 0)

    def out_copy(e, n, slot):
        return pltpu.make_async_remote_copy(
            src_ref=pieces.at[e, slot], dst_ref=landed.at[e, me],
            send_sem=out_send.at[e, n], recv_sem=out_recv.at[e, me],
            device_id=peer(slot), device_id_type=MESH,
        )

    def out_arrival(e, slot):
        return pltpu.make_async_remote_copy(
            src_ref=pieces.at[e, slot], dst_ref=landed.at[e, slot],
            send_sem=out_send.at[e, 0], recv_sem=out_recv.at[e, slot],
            device_id=peer(slot), device_id_type=MESH,
        )

    def half(turn, carry):
        e = (q // 2 + turn) % 2
        @pl.when(turn == 1)
        def _():
            for zz in range(2):
                arrival(1, 2 * e + zz).wait_recv()

                @pl.when(core == 1)
                def _():
                    mate_copy(2 * e + zz, 2 * e + zz).start()

        for zz in range(2):
            arrival(0, 2 * e + zz).wait_recv()

        def gather(t, inner):
            columns = pl.ds(pl.multiple_of(t * TILE, TILE), TILE)
            parts = [
                right[k, 2 * e + zz, :, columns].astype(jnp.float32)
                for k in range(ROUNDS)
                for zz in range(2)
            ]
            for sc in range(4):
                rows = jnp.concatenate([p[4 * sc : 4 * sc + 4] for p in parts], axis=0)
                partner[sc, :, columns] = rows.astype(jnp.bfloat16)
            return inner

        lax.fori_loop(0, TILES, gather, 0)

        limit = jnp.zeros((16, LAGS), jnp.int32)
        for k in range(ROUNDS):
            column = jnp.where(flip[k], NY - 1 - y, y)
            for zz in range(2):
                group = (g - 1 - k + NG) % NG
                at = group * (NZ * NY) + (parity + 2 * (2 * e + zz)) * NY + column
                least = jnp.minimum(counts[0, at], counts[1, at])
                limit = jnp.where(row_id // 4 == k * 2 + zz, least, limit)
        both = jnp.where(row_id % 4 < limit, 0.5, 0.0).astype(jnp.float32)

        def owners(n, inner):
            first = turn == 0
            pair = (y // 2 + 1 + n) % 2
            side = (parity + n) % 2
            slots = [
                jnp.where(first, side * NY + i, (i // 2) * NY + pair * 2 + i % 2)
                for i in range(OWNERS)
            ]

            @pl.when(jnp.logical_and(first, n == 1))
            def _():
                lax.fori_loop(NY, PEERS, widen, 0)


            def tile(t, acc):
                columns = pl.ds(pl.multiple_of(t * TILE, TILE), TILE)
                a0, b0, a1, b1 = [partner[sc, :, columns] for sc in range(4)]
                products = []
                for slot in slots:
                    for ch in range(CH):
                        ma0, mb0, ma1, mb1 = [
                            left_wide[slot * 16 + 4 * sc + ch, :, columns] for sc in range(4)
                        ]
                        real = (ma0 * a0 + mb0 * b0) + (ma1 * a1 + mb1 * b1)
                        imag = (mb0 * a0 - ma0 * b0) + (mb1 * a1 - ma1 * b1)
                        products.append(jnp.concatenate([real, imag], axis=1))
                rows = pl.ds(pl.multiple_of(t * 2 * TILE, 2 * TILE), 2 * TILE)
                return acc + jnp.dot(
                    jnp.concatenate(products, axis=0),
                    table[rows, :],
                    preferred_element_type=jnp.float32,
                )

            lagged = lax.fori_loop(
                0, TILES, tile, jnp.zeros((OWNERS * CH * 16, LAGS), jnp.float32), unroll=2
            )
            for i, slot in enumerate(slots):
                at = g * (NZ * NY) + (2 * q + slot // NY) * NY + slot % NY
                least = jnp.minimum(counts[0, at], counts[1, at])
                for ch in range(CH):
                    factor = jnp.where(least > ch, 1.0, 0.0).astype(jnp.float32)
                    at_row = (i * CH + ch) * 16
                    pieces[e, slot, ch] = (
                        lagged[at_row : at_row + 16] * (1.0 - both * factor)
                    ).astype(jnp.bfloat16)
            for i, slot in enumerate(slots):

                @pl.when(slot != me)
                def _():
                    out_copy(e, slot, slot).start()

            return inner

        lax.fori_loop(0, PEERS // OWNERS, owners, 0)
        return carry

    lax.fori_loop(0, 2, half, 0)

    def store(e):
        return pltpu.make_async_copy(
            result.at[:, :, pl.ds(pl.multiple_of(e * 64, 64), 64), :],
            out_ref.at[:, :, pl.ds(pl.multiple_of(e * 64, 64), 64), :],
            local_sem.at[3 + e],
        )

    for turn in range(2):
        e = (q // 2 + turn) % 2
        for n in range(PEERS - 1):
            out_arrival(e, (me + 1 + n) % PEERS).wait_recv()
        landed[e, me] = pieces[e, me]

        def assemble(n, carry, e=e):
            side = n // CH
            ch = n % CH
            for k in range(ROUNDS):
                parts = []
                for column in range(NY):
                    source = jnp.where(flip[k], NY - 1 - column, column)
                    tile = landed[e, side * NY + source, ch].astype(jnp.float32)
                    parts.append(tile[8 * k : 8 * k + 8])
                for zz in range(2):
                    rows = jnp.concatenate([p[4 * zz : 4 * zz + 4] for p in parts], axis=0)
                    at = pl.multiple_of((side + 4 * e + 2 * zz) * 16, 16)
                    result[k, ch, pl.ds(at, 16), :] = rows.astype(jnp.bfloat16)
            return carry

        lax.fori_loop(0, 2 * CH, assemble, 0)
        store(e).start()

    for n in range(PEERS - 1):
        left_copy(white, me, facing, n).wait_send()
        for e in range(2):
            out_copy(e, (me + 1 + n) % PEERS, facing).wait_send()
    @pl.when(feeds)
    def _():
        feed_copy().wait_send()

    for other in range(4):

        @pl.when(straight(other))
        def _():
            ahead_copy(other, other).wait_send()

        @pl.when(jnp.logical_and(spreads, other // 2 != q // 2))
        def _():
            spread_copy(other).wait_send()

        @pl.when(core == 0)
        def _():
            own_copy(other, other).wait_send()

        @pl.when(core == 1)
        def _():
            mate_copy(other, other).wait_send()

    store(0).wait()
    store(1).wait()


def local(spectra, counts, table):
    bf16 = jnp.bfloat16
    dma = pltpu.SemaphoreType.DMA
    return pl.pallas_call(
        kernel,
        out_shape=jax.ShapeDtypeStruct((ROUNDS, CH, NZ * NY * CH, LAGS), bf16),
        in_specs=[pl.BlockSpec(memory_space=pl.ANY)] * 3,
        out_specs=pl.BlockSpec(memory_space=pl.ANY),
        scratch_shapes=[
            pltpu.VMEM((CH, 2, 2, BINS), jnp.float32),
            pltpu.SMEM(counts.shape, jnp.int32),
            pltpu.VMEM((16, BINS), bf16),
            pltpu.VMEM((16, BINS), bf16),
            pltpu.VMEM((16, BINS), jnp.float32),
            pltpu.VMEM((PEERS, 16, BINS), bf16),
            pltpu.VMEM((PEERS * 16, 16, BINS), bf16),
            pltpu.VMEM((ROUNDS, 4, 16, BINS), bf16),
            pltpu.VMEM((4, 16, BINS), bf16),
            pltpu.VMEM((2 * BINS, LAGS), bf16),
            pltpu.VMEM((2, PEERS, CH, 16, LAGS), bf16),
            pltpu.VMEM((2, PEERS, CH, 16, LAGS), bf16),
            pltpu.VMEM((ROUNDS, CH, NZ * NY * CH, LAGS), bf16),
            dma((5,)),
            pltpu.SemaphoreType.REGULAR((4,)),
            dma((PEERS - 1,)),
            dma((PEERS,)),
            dma((ROUNDS, 4)),
            dma((4,)),
            dma((2,)),
            dma((4,)),
            dma((4,)),
            dma((2, PEERS)),
            dma((2, PEERS)),
        ],
        compiler_params=pltpu.CompilerParams(
            collective_id=0, has_side_effects=True, vmem_limit_bytes=60 * 1024 * 1024
        ),
        cost_estimate=pl.CostEstimate(
            flops=1100000000, bytes_accessed=1600000, transcendentals=0
        ),
    )(spectra, counts, table)


def solution(mesh):
    table = lag_table()

    def whole(spectra, counts):
        return jax.shard_map(
            local,
            mesh=mesh,
            in_specs=(P(("grp", "dev"), None, None, None), P(), P()),
            out_specs=P(None, ("grp", "dev"), None, None),
            check_vma=False,
        )(spectra, counts, jnp.asarray(table))

    return whole
```

```python
import math

import jax
import jax.numpy as jnp
import ml_dtypes
import numpy as np
from jax import lax
from jax.experimental import pallas as pl
from jax.experimental.pallas import tpu as pltpu
from jax.sharding import PartitionSpec as P

LAGS = 128
ROUNDS = 2
NZ = 8
NY = 4
NG = 16
NX = 4
CH = 4
BINS = 2048
TILE = 512
TILES = BINS // TILE
PEERS = 2 * NY
OWNERS = 4
MESH = pl.DeviceIdType.MESH


def lag_table():
    frequency = np.arange(BINS, dtype=np.int64)
    lag_index = np.arange(LAGS, dtype=np.int64) - LAGS // 2
    turns = np.mod(frequency[:, None] * lag_index[None, :], 2 * BINS)
    angles = turns * (math.pi / BINS)
    table = np.stack([np.cos(angles), -np.sin(angles)], 0) / math.sqrt(BINS)
    table = table.reshape(2, TILES, TILE, LAGS).transpose(1, 0, 2, 3).reshape(2 * BINS, LAGS)
    return table.astype(np.float32).astype(ml_dtypes.bfloat16)


def kernel(
    spectra_ref, counts_hbm, table_ref, out_ref,
    raw, counts, white, fed, wide_f32, left, left_wide, right, partner, table, pieces, landed, result,
    local_sem, reply_sem, left_send, left_recv, right_recv, ahead_send, feed_sem, spread_send, mate_send,
    out_send, out_recv,
):
    g = lax.axis_index("grp")
    d = lax.axis_index("dev")
    z = d // NY
    y = d % NY
    core = g % 2
    x = (g // 2) % NX
    parity = z % 2
    q = z // 2
    me = parity * NY + y
    mate_g = g + 1 - 2 * core

    load_raw = pltpu.make_async_copy(spectra_ref, raw, local_sem.at[0])
    load_raw.start()
    load_counts = pltpu.make_async_copy(counts_hbm, counts, local_sem.at[1])
    load_counts.start()
    load_table = pltpu.make_async_copy(table_ref, table, local_sem.at[2])
    load_table.start()

    def peer(slot):
        return (g, (2 * q + slot // NY) * NY + slot % NY)

    def row(other_q, group):
        return (group, (parity + 2 * other_q) * NY + y)

    late = q >= 2
    beside = q + 1 - 2 * (q % 2)
    mate = (mate_g, d)
    column_to = jnp.where(x == NX - 1, NY - 1 - y, y)
    column_from = jnp.where(x == 0, NY - 1 - y, y)

    def ahead(other_q):
        return ((g + 2) % NG, (parity + 2 * other_q) * NY + column_to)

    feeds = jnp.logical_and(x == NX - 1, core == 0)
    spreads = jnp.logical_and(x == 0, core == 0)
    fed_by = ((g + 6) % NG, d)
    feed_to = ((g + 10) % NG, d)

    def behind(other_q):
        spread = jnp.logical_and(spreads, other_q // 2 != q // 2)
        group = jnp.where(spread, g + 8, g - 2 + NG) % NG
        return (group, (parity + 2 * other_q) * NY + column_from)

    barrier = pltpu.get_barrier_semaphore()

    def greet(device, semaphore=barrier):
        pl.semaphore_signal(semaphore, inc=1, device_id=device, device_id_type=MESH)

    @pl.when(jnp.logical_not(late))
    def _():
        for other in (2, 3):
            greet(behind(other))
            greet(row(other, mate_g))

        @pl.when(jnp.logical_not(feeds))
        def _():
            for other in (2, 3):
                greet(ahead(other))

    @pl.when(spreads)
    def _():
        greet(fed_by)

    greet(behind(q))
    greet(behind(beside))
    greet(mate)
    greet(row(beside, mate_g))
    for step in range(1, PEERS):
        greet(peer((me + step) % PEERS))
    near = 4 + PEERS - 1 + jnp.where(feeds, 1, 0)

    load_counts.wait()
    load_raw.wait()
    block = g * (NZ * NY) + d
    for ch in range(CH):
        for s in range(2):
            values = raw[ch, s]
            square = values * values
            lanes = square[:, 0:128]
            for t in range(1, BINS // 128):
                lanes = lanes + square[:, t * 128 : (t + 1) * 128]
            total = jnp.sum(jnp.sum(lanes, axis=0, keepdims=True), axis=1, keepdims=True)
            live = jnp.where(counts[s, block] > ch, 1.0, 0.0).astype(jnp.float32)
            scale = live / jnp.sqrt(total * (1.0 / (2 * BINS)) + 1e-06)
            wide_f32[s * 8 + ch : s * 8 + ch + 1, :] = values[0:1] * scale
            wide_f32[s * 8 + 4 + ch : s * 8 + 4 + ch + 1, :] = values[1:2] * scale
    white[...] = wide_f32[...].astype(jnp.bfloat16)

    @pl.when(jnp.logical_not(late))
    def _():
        pl.semaphore_wait(barrier, near)

    @pl.when(late)
    def _():
        pl.semaphore_wait(barrier, near + 6 - jnp.where(feeds, 2, 0))
        for other in (0, 1):
            greet(behind(other), reply_sem.at[q])
            greet(row(other, mate_g), reply_sem.at[q])

    def ahead_copy(n, other):
        return pltpu.make_async_remote_copy(
            src_ref=white, dst_ref=right.at[1, q],
            send_sem=ahead_send.at[n], recv_sem=right_recv.at[1, q],
            device_id=ahead(other), device_id_type=MESH,
        )

    def own_copy(n, other):
        return pltpu.make_async_remote_copy(
            src_ref=white, dst_ref=right.at[0, q],
            send_sem=mate_send.at[n], recv_sem=right_recv.at[0, q],
            device_id=row(other, mate_g), device_id_type=MESH,
        )

    def mate_copy(n, other):
        return pltpu.make_async_remote_copy(
            src_ref=right.at[1, other], dst_ref=right.at[0, other],
            send_sem=mate_send.at[n], recv_sem=right_recv.at[0, other],
            device_id=mate, device_id_type=MESH,
        )

    def arrival(k, other):
        return pltpu.make_async_remote_copy(
            src_ref=white, dst_ref=right.at[k, other],
            send_sem=ahead_send.at[0], recv_sem=right_recv.at[k, other],
            device_id=mate, device_id_type=MESH,
        )

    facing = (PEERS // 2 + me) % PEERS

    def left_copy(source, slot, target, n):
        return pltpu.make_async_remote_copy(
            src_ref=source, dst_ref=left.at[slot],
            send_sem=left_send.at[n], recv_sem=left_recv.at[slot],
            device_id=peer(target), device_id_type=MESH,
        )

    def in_row(n):
        flipped = y + 1 - 2 * (y % 2)
        return parity * NY + (flipped if n == 1 else (y + 2) % NY if n == 2 else (flipped + 2) % NY)

    def feed_copy():
        return pltpu.make_async_remote_copy(
            src_ref=white, dst_ref=fed, send_sem=feed_sem.at[0], recv_sem=feed_sem.at[1],
            device_id=feed_to, device_id_type=MESH,
        )

    def spread_copy(other):
        return pltpu.make_async_remote_copy(
            src_ref=fed, dst_ref=right.at[1, q],
            send_sem=spread_send.at[other], recv_sem=right_recv.at[1, q],
            device_id=behind(other), device_id_type=MESH,
        )

    def straight(other):
        return jnp.logical_or(jnp.logical_not(feeds), other // 2 == q // 2)

    def send_row(other):
        @pl.when(straight(other))
        def _():
            ahead_copy(other, other).start()

        @pl.when(core == 0)
        def _():
            own_copy(other, other).start()

    @pl.when(feeds)
    def _():
        feed_copy().start()

    @pl.when(late)
    def _():
        for other in (0, 1):
            send_row(other)

    for n in range(1, NY):
        left_copy(white, me, in_row(n), n).start()
    left_copy(white, me, facing, 0).start()
    send_row(q)
    send_row(beside)

    def left_arrival(slot):
        left_copy(white, slot, facing, 0).wait_recv()

    @pl.when(jnp.logical_and(spreads, late))
    def _():
        feed_copy().wait_recv()
        spread_copy(0).start()
        spread_copy(1).start()

    for n in range(1, NY):
        left_arrival(in_row(n))
        left_copy(left.at[in_row(n)], in_row(n), facing, NY - 1 + n).start()

    @pl.when(jnp.logical_not(late))
    def _():
        @pl.when(spreads)
        def _():
            feed_copy().wait_recv()

        for other in (2, 3):
            pl.semaphore_wait(
                reply_sem.at[other], 2 + jnp.where(spreads, 1, 0) - jnp.where(feeds, 1, 0)
            )
            send_row(other)

            @pl.when(spreads)
            def _():
                spread_copy(other).start()

    for other in (q, beside):
        arrival(1, other).wait_recv()

        @pl.when(core == 1)
        def _():
            mate_copy(other, other).start()

    def widen(n, carry):
        row_first = jnp.where(n < NY, parity, 1 - parity) * NY
        slot = row_first + (y + n) % NY

        @pl.when(n >= NY)
        def _():
            left_arrival(slot)

        @pl.when(n > 0)
        def _():
            wide_f32[...] = left[slot].astype(jnp.float32)

        def tile(t, inner):
            columns = pl.ds(pl.multiple_of(t * TILE, TILE), TILE)
            for r in range(16):
                left_wide[slot * 16 + r, :, columns] = jnp.broadcast_to(
                    wide_f32[r : r + 1, columns], (16, TILE)
                ).astype(jnp.bfloat16)
            return inner

        lax.fori_loop(0, TILES, tile, 0)
        return carry

    lax.fori_loop(0, NY, widen, 0)
    load_table.wait()

    mirror = x == 0
    flip = [jnp.logical_and(mirror, core == 0), mirror]
    row_id = lax.broadcasted_iota(jnp.int32, (16, LAGS), 0)

    def out_copy(e, n, slot):
        return pltpu.make_async_remote_copy(
            src_ref=pieces.at[e, slot], dst_ref=landed.at[e, me],
            send_sem=out_send.at[e, n], recv_sem=out_recv.at[e, me],
            device_id=peer(slot), device_id_type=MESH,
        )

    def out_arrival(e, slot):
        return pltpu.make_async_remote_copy(
            src_ref=pieces.at[e, slot], dst_ref=landed.at[e, slot],
            send_sem=out_send.at[e, 0], recv_sem=out_recv.at[e, slot],
            device_id=peer(slot), device_id_type=MESH,
        )

    def half(turn, carry):
        e = (q // 2 + turn) % 2
        @pl.when(turn == 1)
        def _():
            for zz in range(2):
                arrival(1, 2 * e + zz).wait_recv()

                @pl.when(core == 1)
                def _():
                    mate_copy(2 * e + zz, 2 * e + zz).start()

        for zz in range(2):
            arrival(0, 2 * e + zz).wait_recv()

        def gather(t, inner):
            columns = pl.ds(pl.multiple_of(t * TILE, TILE), TILE)
            parts = [
                right[k, 2 * e + zz, :, columns].astype(jnp.float32)
                for k in range(ROUNDS)
                for zz in range(2)
            ]
            for sc in range(4):
                rows = jnp.concatenate([p[4 * sc : 4 * sc + 4] for p in parts], axis=0)
                partner[sc, :, columns] = rows.astype(jnp.bfloat16)
            return inner

        lax.fori_loop(0, TILES, gather, 0)

        limit = jnp.zeros((16, LAGS), jnp.int32)
        for k in range(ROUNDS):
            column = jnp.where(flip[k], NY - 1 - y, y)
            for zz in range(2):
                group = (g - 1 - k + NG) % NG
                at = group * (NZ * NY) + (parity + 2 * (2 * e + zz)) * NY + column
                least = jnp.minimum(counts[0, at], counts[1, at])
                limit = jnp.where(row_id // 4 == k * 2 + zz, least, limit)
        both = jnp.where(row_id % 4 < limit, 0.5, 0.0).astype(jnp.float32)

        def owners(n, inner):
            first = turn == 0
            pair = (y // 2 + 1 + n) % 2
            side = (parity + n) % 2
            slots = [
                jnp.where(first, side * NY + i, (i // 2) * NY + pair * 2 + i % 2)
                for i in range(OWNERS)
            ]

            @pl.when(jnp.logical_and(first, n == 1))
            def _():
                lax.fori_loop(NY, PEERS, widen, 0)


            def tile(t, acc):
                columns = pl.ds(pl.multiple_of(t * TILE, TILE), TILE)
                a0, b0, a1, b1 = [partner[sc, :, columns] for sc in range(4)]
                products = []
                for slot in slots:
                    for ch in range(CH):
                        ma0, mb0, ma1, mb1 = [
                            left_wide[slot * 16 + 4 * sc + ch, :, columns] for sc in range(4)
                        ]
                        real = (ma0 * a0 + mb0 * b0) + (ma1 * a1 + mb1 * b1)
                        imag = (mb0 * a0 - ma0 * b0) + (mb1 * a1 - ma1 * b1)
                        products.append(jnp.concatenate([real, imag], axis=1))
                rows = pl.ds(pl.multiple_of(t * 2 * TILE, 2 * TILE), 2 * TILE)
                return acc + jnp.dot(
                    jnp.concatenate(products, axis=0),
                    table[rows, :],
                    preferred_element_type=jnp.float32,
                )

            lagged = lax.fori_loop(
                0, TILES, tile, jnp.zeros((OWNERS * CH * 16, LAGS), jnp.float32), unroll=2
            )
            for i, slot in enumerate(slots):
                at = g * (NZ * NY) + (2 * q + slot // NY) * NY + slot % NY
                least = jnp.minimum(counts[0, at], counts[1, at])
                for ch in range(CH):
                    factor = jnp.where(least > ch, 1.0, 0.0).astype(jnp.float32)
                    at_row = (i * CH + ch) * 16
                    pieces[e, slot, ch] = (
                        lagged[at_row : at_row + 16] * (1.0 - both * factor)
                    ).astype(jnp.bfloat16)
            for i, slot in enumerate(slots):

                @pl.when(slot != me)
                def _():
                    out_copy(e, slot, slot).start()

            return inner

        lax.fori_loop(0, PEERS // OWNERS, owners, 0)
        return carry

    lax.fori_loop(0, 2, half, 0)

    def store(e):
        return pltpu.make_async_copy(
            result.at[:, :, pl.ds(pl.multiple_of(e * 64, 64), 64), :],
            out_ref.at[:, :, pl.ds(pl.multiple_of(e * 64, 64), 64), :],
            local_sem.at[3 + e],
        )

    for turn in range(2):
        e = (q // 2 + turn) % 2
        for n in range(PEERS - 1):
            out_arrival(e, (me + 1 + n) % PEERS).wait_recv()
        landed[e, me] = pieces[e, me]

        def assemble(n, carry, e=e):
            side = n // CH
            ch = n % CH
            for k in range(ROUNDS):
                parts = []
                for column in range(NY):
                    source = jnp.where(flip[k], NY - 1 - column, column)
                    tile = landed[e, side * NY + source, ch].astype(jnp.float32)
                    parts.append(tile[8 * k : 8 * k + 8])
                for zz in range(2):
                    rows = jnp.concatenate([p[4 * zz : 4 * zz + 4] for p in parts], axis=0)
                    at = pl.multiple_of((side + 4 * e + 2 * zz) * 16, 16)
                    result[k, ch, pl.ds(at, 16), :] = rows.astype(jnp.bfloat16)
            return carry

        lax.fori_loop(0, 2 * CH, assemble, 0)
        store(e).start()

    for n in range(PEERS - 1):
        left_copy(white, me, facing, n).wait_send()
        for e in range(2):
            out_copy(e, (me + 1 + n) % PEERS, facing).wait_send()
    @pl.when(feeds)
    def _():
        feed_copy().wait_send()

    for other in range(4):

        @pl.when(straight(other))
        def _():
            ahead_copy(other, other).wait_send()

        @pl.when(jnp.logical_and(spreads, other // 2 != q // 2))
        def _():
            spread_copy(other).wait_send()

        @pl.when(core == 0)
        def _():
            own_copy(other, other).wait_send()

        @pl.when(core == 1)
        def _():
            mate_copy(other, other).wait_send()

    store(0).wait()
    store(1).wait()


def local(spectra, counts, table):
    bf16 = jnp.bfloat16
    dma = pltpu.SemaphoreType.DMA
    return pl.pallas_call(
        kernel,
        out_shape=jax.ShapeDtypeStruct((ROUNDS, CH, NZ * NY * CH, LAGS), bf16),
        in_specs=[pl.BlockSpec(memory_space=pl.ANY)] * 3,
        out_specs=pl.BlockSpec(memory_space=pl.ANY),
        scratch_shapes=[
            pltpu.VMEM((CH, 2, 2, BINS), jnp.float32),
            pltpu.SMEM(counts.shape, jnp.int32),
            pltpu.VMEM((16, BINS), bf16),
            pltpu.VMEM((16, BINS), bf16),
            pltpu.VMEM((16, BINS), jnp.float32),
            pltpu.VMEM((PEERS, 16, BINS), bf16),
            pltpu.VMEM((PEERS * 16, 16, BINS), bf16),
            pltpu.VMEM((ROUNDS, 4, 16, BINS), bf16),
            pltpu.VMEM((4, 16, BINS), bf16),
            pltpu.VMEM((2 * BINS, LAGS), bf16),
            pltpu.VMEM((2, PEERS, CH, 16, LAGS), bf16),
            pltpu.VMEM((2, PEERS, CH, 16, LAGS), bf16),
            pltpu.VMEM((ROUNDS, CH, NZ * NY * CH, LAGS), bf16),
            dma((5,)),
            pltpu.SemaphoreType.REGULAR((4,)),
            dma((PEERS - 1,)),
            dma((PEERS,)),
            dma((ROUNDS, 4)),
            dma((4,)),
            dma((2,)),
            dma((4,)),
            dma((4,)),
            dma((2, PEERS)),
            dma((2, PEERS)),
        ],
        compiler_params=pltpu.CompilerParams(
            collective_id=0, has_side_effects=True, vmem_limit_bytes=60 * 1024 * 1024
        ),
        cost_estimate=pl.CostEstimate(
            flops=1100000000, bytes_accessed=1600000, transcendentals=0
        ),
    )(spectra, counts, table)


def solution(mesh):
    table = lag_table()

    def whole(spectra, counts):
        return jax.shard_map(
            local,
            mesh=mesh,
            in_specs=(P(("grp", "dev"), None, None, None), P(), P()),
            out_specs=P(None, ("grp", "dev"), None, None),
            check_vma=False,
        )(spectra, counts, jnp.asarray(table))

    return whole
```
